256 devices in a mesh: ctx: 2 (over x_hi), tok: 16 (over z, core), head: 8 (over y, x_lo).
Axes of the slice: x: 4 (x_hi: 2, x_lo: 2; x = x_hi * 2 + x_lo), y: 4, z: 8, core: 2. Of those that a mesh axis runs over, the one named last changes fastest.
Arguments:
- keys: bfloat16 [2, 2, 16, 12288, 256], P(None, 'ctx', 'head', 'tok'), may hold values from -6 to 6
- values: bfloat16 [2, 2, 16, 12288, 256], P(None, 'ctx', 'head', 'tok'), may hold values from -6 to 6
- queries: bfloat16 [2, 2, 16, 12288, 256], P(None, 'ctx', 'head', 'tok'), may hold values from -6 to 6
- rates: float32 [2, 2, 16, 12288], P(None, 'ctx', 'head', 'tok'), may hold values from 0.1 to 3, as said below
- state_in: bfloat16 [2, 16, 3, 256, 512], P('ctx', 'head'), may hold values from -0.375 to 0.375
- fresh: bfloat16 [16, 3, 256, 512], P('head'), may hold values from -0.375 to 0.375
Outputs:
- outputs: bfloat16 [2, 2, 16, 12288, 256], P(None, 'ctx', 'head', 'tok')
The draws below stay inside these ranges and needn't reach their ends.
Inputs may be any that keep to these rules, and one draw needn't show every extreme that they name: Positive per-token learning rates.
All inputs are finite; a program needn't handle non-finite values.
Results may differ from the reference program's by a relative error of at most 0.023.
Values may be sent and summed in bfloat16 or wider, within the bound.
A program may use at most 64 MiB of HBM per device.

```python
import jax
import jax.numpy as jnp
from jax import lax

DH = 256
DF = 512
TOK_DEV = 768
HEADS = 16
SPAN = 12288
SPANS = 2
N_TOK = 16


def draw_rates(key, part):
    shape = (2, SPANS, HEADS, SPAN)
    base = jnp.exp(jax.random.uniform(key, shape, jnp.float32, jnp.log(0.1), 0.0))
    rise = 3.0 ** (jnp.arange(HEADS, dtype=jnp.float32) / max(HEADS - 1, 1))
    return base * rise[None, None, :, None]


def block_scale(key, dims, cuts, smallest, top_value):
    def one(dim, blocks):
        draws = jax.random.uniform(jax.random.fold_in(jax.random.fold_in(key, 6), dim), (blocks,), jnp.float32, smallest / len(cuts), top_value / len(cuts))
        return jnp.repeat(jnp.exp(draws), dims[dim] // blocks).reshape((-1,) + (1,) * (len(dims) - dim - 1))

    factor_of = one(*cuts[0])
    for cut in cuts[1:]:
        factor_of = factor_of * one(*cut)
    return factor_of


def gaussian(key, shape, scale, bound, pieces=(), kind=jnp.bfloat16):
    array = jax.random.normal(key, shape, jnp.float32) * scale
    if len(pieces) > 0:
        array = block_scale(key, shape, pieces, -0.22, 0.18) * array
    return jnp.clip(array, min=-bound, max=bound).astype(kind)


def setup_inputs(seed: int = 0) -> dict:
    splits = jax.random.split(jax.random.key(seed), 7)
    keys = gaussian(splits[0], (2, SPANS, HEADS, SPAN, DH), 1.0, 6.0, ((1, 2), (2, 8), (3, 16)))
    values = gaussian(splits[1], (2, SPANS, HEADS, SPAN, DH), 1.0, 6.0, ((1, 2), (2, 8), (3, 16)))
    queries = gaussian(splits[2], (2, SPANS, HEADS, SPAN, DH), 1.0, 6.0, ((1, 2), (2, 8), (3, 16)))
    rates = draw_rates(jax.random.fold_in(splits[6], 71), 0)
    state_in = gaussian(splits[4], (SPANS, HEADS, 3, DH, DF), DH ** -0.5, 0.375, ((0, 2), (1, 8)))
    fresh = gaussian(splits[5], (HEADS, 3, DH, DF), DH ** -0.5, 0.375, ((0, 8),))
    return {"keys": keys, "values": values, "queries": queries, "rates": rates, "state_in": state_in, "fresh": fresh}


def partial_grads(state, keys_p, values_p, rate_p):
    w_one = state[0]
    w_three = state[1]
    w_back = state[2]
    h_one = jnp.dot(keys_p, w_one, preferred_element_type=jnp.float32)
    h_three = jnp.dot(keys_p, w_three, preferred_element_type=jnp.float32)
    sig = jax.nn.sigmoid(h_one)
    act = (h_one * sig * h_three).astype(jnp.bfloat16)
    weighted = (rate_p[:, None] * values_p.astype(jnp.float32)).astype(jnp.bfloat16)
    dact = -jnp.dot(weighted, w_back, preferred_element_type=jnp.float32)
    d_one = (dact * h_three * sig * (1.0 + h_one * (1.0 - sig))).astype(jnp.bfloat16)
    d_three = (dact * h_one * sig).astype(jnp.bfloat16)
    g_one = jnp.dot(keys_p.T, d_one, preferred_element_type=jnp.float32)
    g_three = jnp.dot(keys_p.T, d_three, preferred_element_type=jnp.float32)
    g_back = -jnp.dot(weighted.T, act, preferred_element_type=jnp.float32)
    return jnp.stack([g_one, g_three, g_back])

def head_grads(state, keys_h, values_h, rates_h):
    total = jnp.zeros(state.shape, jnp.float32)
    for piece in range(N_TOK):
        lo = piece * TOK_DEV
        part_grad = partial_grads(state, keys_h[lo:lo + TOK_DEV], values_h[lo:lo + TOK_DEV], rates_h[lo:lo + TOK_DEV])
        part_grad = lax.optimization_barrier(part_grad.astype(jnp.bfloat16))
        total = total + part_grad.astype(jnp.float32)
    return total

def apply_state(state, queries_h):
    p_one = jnp.dot(queries_h, state[0], preferred_element_type=jnp.float32)
    p_three = jnp.dot(queries_h, state[1], preferred_element_type=jnp.float32)
    mixed = (jax.nn.silu(p_one) * p_three).astype(jnp.bfloat16)
    return jnp.dot(mixed, state[2].T, preferred_element_type=jnp.float32).astype(jnp.bfloat16)

def update_block(states, keys_c, values_c, rates_c):
    grads = jax.vmap(head_grads)(states, keys_c, values_c, rates_c)
    total_sq = jnp.sum(grads * grads)
    scale = 0.5 * jnp.sqrt(jnp.float32(3 * DF * HEADS)) / jnp.sqrt(total_sq + 1e-06)
    older = states.astype(jnp.float32)
    moved = older - scale * grads
    old_norm = jnp.sqrt(lax.optimization_barrier(jnp.sum(older * older, axis=-2, keepdims=True)))
    new_norm = jnp.sqrt(lax.optimization_barrier(jnp.sum(moved * moved, axis=-2, keepdims=True)) + 1e-06)
    return (moved * old_norm / new_norm).astype(jnp.bfloat16)

def reference(keys, values, queries, rates, state_in, fresh):
    first_states = []
    first_outs = []
    for block in range(SPANS):
        newer = update_block(state_in[block], keys[0, block], values[0, block], rates[0, block])
        first_states.append(newer)
        first_outs.append(jax.vmap(apply_state)(newer, queries[0, block]))
    second_outs = []
    for block in range(SPANS):
        incoming = fresh if block == 0 else first_states[block - 1]
        newer = update_block(incoming, keys[1, block], values[1, block], rates[1, block])
        second_outs.append(jax.vmap(apply_state)(newer, queries[1, block]))
    return jnp.stack([jnp.stack(first_outs), jnp.stack(second_outs)])
```

```python
import functools

import jax
import jax.numpy as jnp
from jax import lax
from jax.experimental import pallas as pl
from jax.experimental.pallas import tpu as pltpu
from jax.sharding import PartitionSpec as P

MESH = pl.DeviceIdType.MESH
F32, BF16 = jnp.float32, jnp.bfloat16
NT = (((1,), (1,)), ((), ()))


def sigmoid(x):
    return 0.5 * jnp.tanh(0.5 * x) + 0.5


def kernel(
    sizes,
    keys, values, queries, rates, state_in, fresh,
    out,
    k0, v0, k1, v1, qs, os_, rt, rtp, s0, so, s1, s2, s3,
    kt0, rv0, rvt0, kt1, rv1, rvt1, act, d1, d3,
    gx, gxr, gb, gg, rin, rhalf, rout,
    sqp, sqs, sqz, sqo,
    load_sem, osem, xs, xr, gxs, gxrs, rs_s, rs_r, ag_s, ag_r, ho_s, ho_r, st_s, st_r,
    pp_s, pp_r, zz_s, zz_r, zo_s, zo_r, os_s, os_r,
):
    nz, nh, tok, dh, df, heads_all = sizes
    rows = dh // nz
    half = rows // 2
    c, t, h = lax.axis_index("ctx"), lax.axis_index("tok"), lax.axis_index("head")
    z, core = t // 2, t % 2
    other = 1 - core
    np_ = 2 * nh
    me_p = h * 2 + core

    def zdev(step):
        return (c, lax.rem(z + step + nz, nz) * 2 + core, h)

    def pdev(j):
        p = lax.rem(me_p + j, np_)
        return (c, z * 2 + lax.rem(p, 2), p // 2)

    def odev(step):
        return (1 - c, lax.rem(z + step, nz) * 2 + core, h)

    mate = (c, z * 2 + other, h)
    twin = (1 - c, t, h)

    local = [
        (keys.at[0, 0, other], k0.at[1]),
        (state_in.at[0, other], s0.at[1]),
        (values.at[0, 0, other], v0.at[1]),
        (rates, rt),
        (keys.at[0, 0, core], k0.at[0]),
        (state_in.at[0, core], s0.at[0]),
        (values.at[0, 0, core], v0.at[0]),
        (keys.at[1, 0, core], k1.at[0]),
        (values.at[1, 0, core], v1.at[0]),
        (queries.at[0, 0, core], qs.at[0, 0]),
        (queries.at[1, 0, core], qs.at[1, 0]),
    ]
    loads = [pltpu.make_async_copy(a, b, load_sem.at[i]) for i, (a, b) in enumerate(local)]
    for cp in loads:
        cp.start()
    fresh_load = pltpu.make_async_copy(fresh.at[core], s2, load_sem.at[len(local)])

    @pl.when(c == 0)
    def _():
        fresh_load.start()

    barrier = pltpu.get_barrier_semaphore()
    for j in range(1, np_):
        pl.semaphore_signal(barrier, inc=1, device_id=pdev(j), device_id_type=MESH)
    for j in range(1, nz):
        pl.semaphore_signal(barrier, inc=1, device_id=zdev(j), device_id_type=MESH)
    for j in range(nz):
        pl.semaphore_signal(barrier, inc=1, device_id=odev(j), device_id_type=MESH)

    def remote(src, dst, ss, rs, dev):
        return pltpu.make_async_remote_copy(
            src_ref=src, dst_ref=dst, send_sem=ss, recv_sem=rs, device_id=dev, device_id_type=MESH
        )

    def rate_columns(ref, tick, head):
        row = jnp.where(head == 0, ref[tick, 0, 0:1, :], ref[tick, 0, 1:2, :])
        col = jnp.broadcast_to(row, (128, tok)).T
        return jnp.concatenate([col] * (dh // 128), axis=1)

    def prepare(k, v, col, kt, rv, rvt, lo):
        kt[:, lo:lo + tok] = k[...].T
        weighted = (v[...].astype(F32) * col).astype(BF16)
        rv[lo:lo + tok, :] = weighted
        rvt[:, lo:lo + tok] = weighted.T

    def forward(k, rv, state, lo):
        tile = 256
        for i in range(tok // tile):
            a = lo + i * tile
            kk = k[i * tile:(i + 1) * tile, :]
            h1 = jnp.dot(kk, state[0], preferred_element_type=F32)
            h3 = jnp.dot(kk, state[1], preferred_element_type=F32)
            dact = jnp.dot(rv[a:a + tile, :], state[2], preferred_element_type=F32)
            sig = sigmoid(h1)
            hs = h1 * sig
            act[a:a + tile, :] = (hs * h3).astype(BF16)
            d3[a:a + tile, :] = (dact * hs).astype(BF16)
            d1[a:a + tile, :] = (dact * h3 * (sig + hs * (1.0 - sig))).astype(BF16)

    def grad(m, kt, rvt, lo, hi):
        left, right = ((kt, d1), (kt, d3), (rvt, act))[m]
        return jnp.dot(left[:, lo:hi], right[lo:hi, :], preferred_element_type=F32)

    order = (2, 0, 1)

    for i in (0, 1, 2, 3):
        loads[i].wait()
    prepare(k0.at[1], v0.at[1], rate_columns(rt, 0, other), kt0, rv0, rvt0, 0)
    forward(k0.at[1], rv0, s0.at[1], 0)
    for m in order:
        gx[m] = grad(m, kt0, rvt0, 0, tok).astype(BF16)

    pl.semaphore_wait(barrier, np_ - 1 + nz - 1 + nz)

    gx_copies = {m: remote(gx.at[m], gxr.at[m], gxs.at[m], gxrs.at[m], mate) for m in order}
    for m in order:
        gx_copies[m].start()
    state_copy = remote(s0.at[0], so, st_s, st_r, twin)
    for i in (4, 5, 6):
        loads[i].wait()

    @pl.when(c == 0)
    def _():
        state_copy.start()

    mate_copies = [
        remote(src, dst, xs.at[i], xr.at[i], mate)
        for i, (src, dst) in enumerate([
            (rates, rtp),
            (keys.at[1, 0, other], k1.at[1]),
            (values.at[1, 0, other], v1.at[1]),
            (queries.at[0, 0, other], qs.at[0, 1]),
            (queries.at[1, 0, other], qs.at[1, 1]),
        ])
    ]
    for cp in mate_copies:
        cp.start()

    prepare(k0.at[0], v0.at[0], rate_columns(rt, 0, core), kt0, rv0, rvt0, tok)
    forward(k0.at[0], rv0, s0.at[0], tok)

    def chunk(owner_step, m, part=None):
        owner = lax.rem(z + owner_step + 2 * nz, nz)
        if part is None:
            return (m, pl.ds(pl.multiple_of(owner * rows, rows), rows), slice(None))
        return (m, pl.ds(pl.multiple_of(owner * rows + part * half, half), half), slice(None))

    sides = ((0, -1), (1, 1))

    def rs_copy(tick, hop, d, s, m):
        if hop == 0:
            src, dst, dev = gb.at[(tick,) + chunk(3 * s, m)], rin.at[tick, 0, d, m], zdev(s)
        elif hop == 1:
            src, dst, dev = gb.at[(tick,) + chunk(4, m, d)], rhalf.at[tick, d, m], zdev(2 * s)
        else:
            src, dst, dev = rout.at[tick, hop - 2, d, m], rin.at[tick, hop - 1, d, m], zdev(s)
        return remote(src, dst, rs_s.at[tick, hop, d, m], rs_r.at[tick, hop, d, m], dev)

    def rs_first(tick, m):
        for d, s in sides:
            rs_copy(tick, 1, d, s, m).start()
            rs_copy(tick, 0, d, s, m).start()

    def rs_second(tick, m):
        for d, s in sides:
            rs_copy(tick, 0, d, s, m).wait_recv()
            rs_copy(tick, 1, d, s, m).wait_recv()
            own = gb[(tick,) + chunk(2 * s, m)].astype(F32) + rin[tick, 0, d, m].astype(F32)
            far = rhalf[tick, d, m].astype(F32)
            if d == 0:
                rout[tick, 0, d, m, 0:half, :] = (own[0:half] + far).astype(BF16)
                rout[tick, 0, d, m, half:rows, :] = own[half:rows].astype(BF16)
            else:
                rout[tick, 0, d, m, 0:half, :] = own[0:half].astype(BF16)
                rout[tick, 0, d, m, half:rows, :] = (own[half:rows] + far).astype(BF16)
            rs_copy(tick, 2, d, s, m).start()

    def rs_third(tick, m):
        for d, s in sides:
            rs_copy(tick, 2, d, s, m).wait_recv()
            own = gb[(tick,) + chunk(s, m)].astype(F32) + rin[tick, 1, d, m].astype(F32)
            rout[tick, 1, d, m] = own.astype(BF16)
            rs_copy(tick, 3, d, s, m).start()

    def rs_last(tick, m, buf):
        total = gb[(tick,) + chunk(0, m)].astype(F32)
        for d, s in sides:
            rs_copy(tick, 3, d, s, m).wait_recv()
            total = total + rin[tick, 2, d, m].astype(F32)
        gg[(buf,) + chunk(0, m)] = total.astype(BF16)
        square = total * total
        tile = jnp.zeros((8, 128), F32)
        for i in range(0, rows, 8):
            for j in range(0, df, 128):
                tile = tile + square[i:i + 8, j:j + 128]
        return tile

    def ag_copy(buf, hop, d, s, m):
        if hop == 0:
            part, dev = chunk(0, m), zdev(s)
        elif hop == 1:
            part, dev = chunk(-s, m), zdev(s)
        elif hop == 2:
            part, dev = chunk(-2 * s, m), zdev(s)
        else:
            part, dev = chunk(-2 * s, m, d), zdev(2 * s)
        part = (buf,) + part
        return remote(gg.at[part], gg.at[part], ag_s.at[buf, hop, d, m], ag_r.at[buf, hop, d, m], dev)

    def ag_first(buf, m):
        for d, s in sides:
            ag_copy(buf, 0, d, s, m).start()

    def ag_second(buf, m):
        for d, s in sides:
            ag_copy(buf, 0, d, s, m).wait_recv()
            ag_copy(buf, 1, d, s, m).start()

    def ag_third(buf, m):
        for d, s in sides:
            ag_copy(buf, 1, d, s, m).wait_recv()
            ag_copy(buf, 3, d, s, m).start()
            ag_copy(buf, 2, d, s, m).start()

    def ag_last(buf, m):
        for d, s in sides:
            ag_copy(buf, 3, d, s, m).wait_recv()
            ag_copy(buf, 2, d, s, m).wait_recv()

    def plane_copy(tick, j):
        return remote(sqp.at[tick, me_p], sqp.at[tick, me_p], pp_s.at[tick, j], pp_r.at[tick, j], pdev(j))

    def norm_first(tick, tile):
        sqp[tick, me_p] = tile
        for j in range(1, np_):
            plane_copy(tick, j).start()

    def z_copy(tick, j):
        return remote(sqs.at[tick], sqz.at[tick, z], zz_s.at[tick, j], zz_r.at[tick, j], zdev(j))

    def zo_copy(j):
        return remote(sqs.at[0], sqo.at[z], zo_s.at[j], zo_r.at[j], odev(j))

    def norm_second(tick):
        for j in range(1, np_):
            plane_copy(tick, j).wait_recv()
        total = sqp[tick, 0]
        for j in range(1, np_):
            total = total + sqp[tick, j]
        sqs[tick] = total
        sqz[tick, z] = total
        for j in range(1, nz):
            z_copy(tick, j).start()
        if tick == 0:
            @pl.when(c == 0)
            def _():
                for j in range(nz):
                    zo_copy(j).start()

    def scale_of(ref):
        total = ref[0]
        for j in range(1, nz):
            total = total + ref[j]
        sq = jnp.sum(jnp.sum(total, axis=1, keepdims=True), axis=0, keepdims=True)
        return 0.5 * jnp.sqrt(jnp.float32(3 * df * heads_all)) / jnp.sqrt(sq + 1e-06)

    def renorm(old, buf, scale, new, m):
        for j in range(0, df, 128):
            older = old[m, :, j:j + 128].astype(F32)
            moved = older + scale * gg[buf, m, :, j:j + 128].astype(F32)
            was = jnp.sum(older * older, axis=0, keepdims=True)
            now = jnp.sum(moved * moved, axis=0, keepdims=True)
            factor = jnp.sqrt(was) / jnp.sqrt(now + 1e-06)
            new[m, :, j:j + 128] = (moved * factor).astype(BF16)

    def apply(tick, part, state):
        tile = 256
        for i in range(tok // tile):
            at = slice(i * tile, (i + 1) * tile)
            q = qs[tick, part, at, :]
            p1 = jnp.dot(q, state[0], preferred_element_type=F32)
            p3 = jnp.dot(q, state[1], preferred_element_type=F32)
            pa = (p1 * sigmoid(p1) * p3).astype(BF16)
            os_[tick, part, at, :] = lax.dot_general(pa, state[2], NT, preferred_element_type=F32).astype(BF16)

    def own_out(tick):
        return pltpu.make_async_copy(os_.at[tick, 0], out.at[tick, 0, core], osem.at[tick])

    def mate_out(tick):
        return remote(os_.at[tick, 1], out.at[tick, 0, core], os_s.at[tick], os_r.at[tick], mate)

    for m in order:
        part = grad(m, kt0, rvt0, tok, 2 * tok).astype(BF16).astype(F32)
        gx_copies[m].wait_recv()
        gb[0, m] = (part + gxr[m].astype(F32)).astype(BF16)
        rs_first(0, m)
    loads[7].wait()
    loads[8].wait()
    prepare(k1.at[0], v1.at[0], rate_columns(rt, 1, core), kt1, rv1, rvt1, 0)
    for m in order:
        rs_second(0, m)
    for i in (0, 1, 2):
        mate_copies[i].wait_recv()
    prepare(k1.at[1], v1.at[1], rate_columns(rtp, 1, core), kt1, rv1, rvt1, tok)
    for m in order:
        rs_third(0, m)

    def hand_over(m):
        part = chunk(0, m)
        return remote(gg.at[(0,) + part], gg.at[(1,) + part], ho_s.at[m], ho_r.at[m], twin)

    tile = jnp.zeros((8, 128), F32)
    for m in order:
        tile = tile + rs_last(0, m, 0)

        @pl.when(c == 0)
        def _():
            hand_over(m).start()

        ag_first(0, m)
    norm_first(0, tile)

    @pl.when(c == 1)
    def _():
        for m in order:
            hand_over(m).wait_recv()
            ag_first(1, m)

    norm_second(0)

    @pl.when(c == 1)
    def _():
        for m in order:
            ag_second(1, m)
        for m in order:
            ag_third(1, m)
    for m in order:
        ag_second(0, m)

    @pl.when(c == 1)
    def _():
        for j in range(nz):
            zo_copy(j).wait_recv()
        state_copy.wait_recv()
        scale = scale_of(sqo)
        for m in order:
            ag_last(1, m)
            renorm(so, 1, scale, s2, m)

    @pl.when(c == 0)
    def _():
        fresh_load.wait()

    forward(k1.at[0], rv1, s2, 0)
    for m in order:
        ag_third(0, m)
    forward(k1.at[1], rv1, s2, tok)
    for m in order:
        gb[1, m] = grad(m, kt1, rvt1, 0, 2 * tok).astype(BF16)
        rs_first(1, m)
    for j in range(1, nz):
        z_copy(0, j).wait_recv()
    scale = scale_of(sqz.at[0])
    for m in order:
        ag_last(0, m)
        renorm(s0.at[0], 0, scale, s1, m)
    for m in order:
        rs_second(1, m)
    loads[9].wait()
    mate_copies[3].wait_recv()
    apply(0, 1, s1)
    mate_out(0).start()
    for m in order:
        rs_third(1, m)
    apply(0, 0, s1)
    own_out(0).start()
    tile = jnp.zeros((8, 128), F32)
    for m in order:
        tile = tile + rs_last(1, m, 2)
        ag_first(2, m)
    norm_first(1, tile)
    for m in order:
        ag_second(2, m)
    norm_second(1)
    for m in order:
        ag_third(2, m)
    loads[10].wait()
    mate_copies[4].wait_recv()
    for j in range(1, nz):
        z_copy(1, j).wait_recv()
    scale = scale_of(sqz.at[1])
    for m in order:
        ag_last(2, m)
        renorm(s2, 2, scale, s3, m)
    apply(1, 1, s3)
    mate_out(1).start()
    apply(1, 0, s3)
    own_out(1).start()

    for m in order:
        gx_copies[m].wait_send()
        for tick in (0, 1):
            for hop in range(4):
                for d, s in sides:
                    rs_copy(tick, hop, d, s, m).wait_send()
        for buf in (0, 2):
            for hop in range(4):
                for d, s in sides:
                    ag_copy(buf, hop, d, s, m).wait_send()
    for cp in mate_copies:
        cp.wait_send()
    for tick in (0, 1):
        for j in range(1, np_):
            plane_copy(tick, j).wait_send()
        for j in range(1, nz):
            z_copy(tick, j).wait_send()

    @pl.when(c == 0)
    def _():
        state_copy.wait_send()
        for m in order:
            hand_over(m).wait_send()
        for j in range(nz):
            zo_copy(j).wait_send()

    @pl.when(c == 1)
    def _():
        for m in order:
            for hop in range(4):
                for d, s in sides:
                    ag_copy(1, hop, d, s, m).wait_send()

    for tick in (0, 1):
        own_out(tick).wait()
        mate_out(tick).wait()


def shards(mesh_shape, keys, values, queries, rates, state_in, fresh):
    nz, nh = mesh_shape["tok"] // 2, mesh_shape["head"]
    _, _, _, tok, dh = keys.shape
    df = state_in.shape[-1]
    heads_all = 2 * nh
    rows = dh // nz
    sizes = (nz, nh, tok, dh, df, heads_all)
    dma = pltpu.SemaphoreType.DMA

    def vm(*shape, dtype=BF16):
        return pltpu.VMEM(shape, dtype)

    both = 2 * tok
    state = (3, dh, df)
    scratch = [
        vm(2, tok, dh), vm(2, tok, dh), vm(2, tok, dh), vm(2, tok, dh), vm(2, 2, tok, dh), vm(2, 2, tok, dh),
        vm(*rates.shape, dtype=F32), vm(*rates.shape, dtype=F32),
        vm(2, *state), vm(*state), vm(*state), vm(*state), vm(*state),
        vm(dh, both), vm(both, dh), vm(dh, both), vm(dh, both), vm(both, dh), vm(dh, both),
        vm(both, df), vm(both, df), vm(both, df),
        vm(*state), vm(*state), vm(2, *state), vm(3, *state),
        vm(2, 3, 2, 3, rows, df), vm(2, 2, 3, rows // 2, df), vm(2, 2, 2, 3, rows, df),
        vm(2, 2 * nh, 8, 128, dtype=F32), vm(2, 8, 128, dtype=F32), vm(2, nz, 8, 128, dtype=F32), vm(nz, 8, 128, dtype=F32),
        dma((12,)), dma((2,)), dma((5,)), dma((5,)), dma((3,)), dma((3,)),
        dma((2, 4, 2, 3)), dma((2, 4, 2, 3)), dma((3, 4, 2, 3)), dma((3, 4, 2, 3)),
        dma((3,)), dma((3,)), dma, dma,
        dma((2, 2 * nh)), dma((2, 2 * nh)), dma((2, nz)), dma((2, nz)), dma((nz,)), dma((nz,)),
        dma((2,)), dma((2,)),
    ]
    return pl.pallas_call(
        functools.partial(kernel, sizes),
        out_shape=jax.ShapeDtypeStruct(queries.shape, BF16),
        in_specs=[pl.BlockSpec(memory_space=pl.ANY)] * 6,
        out_specs=pl.BlockSpec(memory_space=pl.ANY),
        scratch_shapes=scratch,
        compiler_params=pltpu.CompilerParams(
            collective_id=0, has_side_effects=True, vmem_limit_bytes=56 * 1024 * 1024
        ),
        cost_estimate=pl.CostEstimate(flops=8_000_000_000, bytes_accessed=10_000_000, transcendentals=3_000_000),
    )(keys, values, queries, rates, state_in, fresh)


def solution(mesh):
    in_specs = (
        P(None, "ctx", "head", "tok", None),
        P(None, "ctx", "head", "tok", None),
        P(None, "ctx", "head", "tok", None),
        P(None, "ctx", "head", "tok"),
        P("ctx", "head", None, None, None),
        P("head", None, None, None),
    )
    return jax.shard_map(
        functools.partial(shards, dict(mesh.shape)),
        mesh=mesh,
        in_specs=in_specs,
        out_specs=P(None, "ctx", "head", "tok", None),
        check_vma=False,
    )
```

```python
import functools

import jax
import jax.numpy as jnp
from jax import lax
from jax.experimental import pallas as pl
from jax.experimental.pallas import tpu as pltpu
from jax.sharding import PartitionSpec as P

MESH = pl.DeviceIdType.MESH
F32, BF16 = jnp.float32, jnp.bfloat16
LANES, GROUP = 128, 256
NT = (((1,), (1,)), ((), ()))


def sigmoid(x):
    return 0.5 * jnp.tanh(0.5 * x) + 0.5


def kernel(
    sizes,
    keys, values, queries, rates, state_in, fresh,
    out,
    k0, v0, k1, v1, qs, os_, rt, rtp, s0, so, s1, s2, s3,
    kt0, rv0, rvt0, kt1, rv1, rvt1, act, d1, d3, pa,
    gx, gxr, gb, gg, rin, rhalf, rout,
    sqp, sqs, sqz, sqo,
    load_sem, xs, xr, gxs, gxrs, rs_s, rs_r, ag_s, ag_r, ho_s, ho_r, st_s, st_r,
    pp_s, pp_r, zz_s, zz_r, zo_s, zo_r, os_s, os_r,
):
    nz, nh, tok, dh, df, heads_all = sizes
    rows = dh // nz
    half = rows // 2
    nb, ng = df // LANES, df // GROUP
    per = nb // ng
    c, t, h = lax.axis_index("ctx"), lax.axis_index("tok"), lax.axis_index("head")
    z, core = t // 2, t % 2
    other = 1 - core
    np_ = 2 * nh
    me_p = h * 2 + core

    def zdev(step):
        return (c, lax.rem(z + step + nz, nz) * 2 + core, h)

    def pdev(j):
        p = lax.rem(me_p + j, np_)
        return (c, z * 2 + lax.rem(p, 2), p // 2)

    def odev(step):
        return (1 - c, lax.rem(z + step, nz) * 2 + core, h)

    mate = (c, z * 2 + other, h)
    twin = (1 - c, t, h)

    local = [
        (keys.at[0, 0, other], k0.at[1]),
        (state_in.at[0, other], s0.at[1]),
        (values.at[0, 0, other], v0.at[1]),
        (rates, rt),
        (keys.at[0, 0, core], k0.at[0]),
        (state_in.at[0, core], s0.at[0]),
        (values.at[0, 0, core], v0.at[0]),
        (keys.at[1, 0, core], k1.at[0]),
        (values.at[1, 0, core], v1.at[0]),
        (queries.at[0, 0, core], qs.at[0, 0]),
        (queries.at[1, 0, core], qs.at[1, 0]),
    ]
    loads = [pltpu.make_async_copy(a, b, load_sem.at[i]) for i, (a, b) in enumerate(local)]
    for i in (0, 1, 2, 3):
        loads[i].start()
    fresh_load = pltpu.make_async_copy(fresh.at[core], s2, load_sem.at[len(local)])

    barrier = pltpu.get_barrier_semaphore()
    for j in range(1, np_):
        pl.semaphore_signal(barrier, inc=1, device_id=pdev(j), device_id_type=MESH)
    for j in range(1, nz):
        pl.semaphore_signal(barrier, inc=1, device_id=zdev(j), device_id_type=MESH)
    for j in range(nz):
        pl.semaphore_signal(barrier, inc=1, device_id=odev(j), device_id_type=MESH)

    def remote(src, dst, ss, rs, dev):
        return pltpu.make_async_remote_copy(
            src_ref=src, dst_ref=dst, send_sem=ss, recv_sem=rs, device_id=dev, device_id_type=MESH
        )

    def rate_columns(ref, tick, head):
        row = jnp.where(head == 0, ref[tick, 0, 0:1, :], ref[tick, 0, 1:2, :])
        col = jnp.broadcast_to(row, (128, tok)).T
        return jnp.concatenate([col] * (dh // 128), axis=1)

    def prepare(k, v, col, kt, rv, rvt, lo):
        kt[:, lo:lo + tok] = k[...].T
        weighted = (v[...].astype(F32) * col).astype(BF16)
        rv[lo:lo + tok, :] = weighted
        rvt[:, lo:lo + tok] = weighted.T

    def forward(k, rv, state, lo, g):
        at, cols = slice(lo, lo + tok), slice(g * GROUP, (g + 1) * GROUP)
        kk = k[...]
        h1 = jnp.dot(kk, state[0, :, cols], preferred_element_type=F32)
        h3 = jnp.dot(kk, state[1, :, cols], preferred_element_type=F32)
        dact = jnp.dot(rv[at, :], state[2, :, cols], preferred_element_type=F32)
        sig = sigmoid(h1)
        hs = h1 * sig
        act[at, cols] = (hs * h3).astype(BF16)
        d3[at, cols] = (dact * hs).astype(BF16)
        d1[at, cols] = (dact * h3 * (sig + hs * (1.0 - sig))).astype(BF16)

    def grad(m, kt, rvt, lo, hi, g):
        left, right = ((kt, d1), (kt, d3), (rvt, act))[m]
        cols = slice(g * GROUP, (g + 1) * GROUP)
        return jnp.dot(left[:, lo:hi], right[lo:hi, cols], preferred_element_type=F32)

    def blocks(g):
        return range(g * per, (g + 1) * per)

    def lanes(b):
        return slice((b % per) * LANES, (b % per + 1) * LANES)

    order = (2, 0, 1)
    everyb = tuple(range(nb))

    for i in (4, 5, 6):
        loads[i].start()
    for i in (0, 1, 2, 3):
        loads[i].wait()
    prepare(k0.at[1], v0.at[1], rate_columns(rt, 0, other), kt0, rv0, rvt0, 0)
    for i in (7, 8, 9, 10):
        loads[i].start()

    @pl.when(c == 0)
    def _():
        fresh_load.start()

    for g in range(ng):
        forward(k0.at[1], rv0, s0.at[1], 0, g)
        for m in order:
            part = grad(m, kt0, rvt0, 0, tok, g).astype(BF16)
            for b in blocks(g):
                gx[b, m] = part[:, lanes(b)]

    pl.semaphore_wait(barrier, np_ - 1 + nz - 1 + nz)

    gx_copies = [
        remote(gx.at[pl.ds(g * per, per)], gxr.at[pl.ds(g * per, per)], gxs.at[g], gxrs.at[g], mate) for g in range(ng)
    ]
    for cp in gx_copies:
        cp.start()
    state_copies = {m: remote(s0.at[0, m], so.at[m], st_s.at[m], st_r.at[m], twin) for m in order}
    for i in (4, 5, 6):
        loads[i].wait()

    @pl.when(c == 0)
    def _():
        state_copies[order[0]].start()
        state_copies[order[1]].start()

    mate_copies = [
        remote(src, dst, xs.at[i], xr.at[i], mate)
        for i, (src, dst) in enumerate([
            (rates, rtp),
            (keys.at[1, 0, other], k1.at[1]),
            (values.at[1, 0, other], v1.at[1]),
            (queries.at[0, 0, other], qs.at[0, 1]),
            (queries.at[1, 0, other], qs.at[1, 1]),
        ])
    ]

    def chunk(owner_step, part=None):
        owner = lax.rem(z + owner_step + 2 * nz, nz)
        if part is None:
            return (slice(None), pl.ds(pl.multiple_of(owner * rows, rows), rows), slice(None))
        return (slice(None), pl.ds(pl.multiple_of(owner * rows + part * half, half), half), slice(None))

    sides = ((0, -1), (1, 1))

    def rs_copy(tick, hop, d, s, b):
        if hop == 0:
            src, dst, dev = gb.at[(tick, b) + chunk(3 * s)], rin.at[tick, 0, d, b], zdev(s)
        elif hop == 1:
            src, dst, dev = gb.at[(tick, b) + chunk(4, d)], rhalf.at[tick, d, b], zdev(3 * s)
        else:
            src, dst, dev = rout.at[tick, hop - 2, d, b], rin.at[tick, hop - 1, d, b], zdev(s)
        return remote(src, dst, rs_s.at[tick, hop, d, b], rs_r.at[tick, hop, d, b], dev)

    def rs_first(tick, b):
        for d, s in sides:
            rs_copy(tick, 0, d, s, b).start()

    def rs_far(tick, b):
        for d, s in sides:
            rs_copy(tick, 1, d, s, b).start()

    def rs_second(tick, b):
        for d, s in sides:
            rs_copy(tick, 0, d, s, b).wait_recv()
            own = gb[(tick, b) + chunk(2 * s)].astype(F32) + rin[tick, 0, d, b].astype(F32)
            rout[tick, 0, d, b] = own.astype(BF16)
            rs_copy(tick, 2, d, s, b).start()

    def rs_third(tick, b):
        for d, s in sides:
            rs_copy(tick, 2, d, s, b).wait_recv()
            rs_copy(tick, 1, d, s, b).wait_recv()
            own = gb[(tick, b) + chunk(s)].astype(F32) + rin[tick, 1, d, b].astype(F32)
            far = rhalf[tick, d, b].astype(F32)
            if d == 0:
                rout[tick, 1, d, b, :, 0:half, :] = (own[:, 0:half] + far).astype(BF16)
                rout[tick, 1, d, b, :, half:rows, :] = own[:, half:rows].astype(BF16)
            else:
                rout[tick, 1, d, b, :, 0:half, :] = own[:, 0:half].astype(BF16)
                rout[tick, 1, d, b, :, half:rows, :] = (own[:, half:rows] + far).astype(BF16)
            rs_copy(tick, 3, d, s, b).start()

    def rs_last(tick, b, buf):
        total = gb[(tick, b) + chunk(0)].astype(F32)
        for d, s in sides:
            rs_copy(tick, 3, d, s, b).wait_recv()
            total = total + rin[tick, 2, d, b].astype(F32)
        gg[(buf, b) + chunk(0)] = total.astype(BF16)
        square = total * total
        tile = jnp.zeros((8, 128), F32)
        for m in range(3):
            for i in range(0, rows, 8):
                tile = tile + square[m, i:i + 8]
        return tile

    def ag_copy(buf, hop, d, s, b):
        if hop == 0:
            part, dev = chunk(0), zdev(s)
        elif hop == 1:
            part, dev = chunk(-s), zdev(s)
        elif hop == 2:
            part, dev = chunk(-2 * s), zdev(s)
        elif buf == 0:
            part, dev = chunk(-3 * s, d), zdev(s)
        else:
            part, dev = chunk(-s, d), zdev(3 * s)
        part = (buf, b) + part
        return remote(gg.at[part], gg.at[part], ag_s.at[buf, hop, d, b], ag_r.at[buf, hop, d, b], dev)

    def ag_first(buf, b):
        for d, s in sides:
            ag_copy(buf, 0, d, s, b).start()

    def ag_second(buf):
        for b in everyb:
            for d, s in sides:
                ag_copy(buf, 0, d, s, b).wait_recv()
                ag_copy(buf, 1, d, s, b).start()
        if buf != 0:
            for b in everyb:
                for d, s in sides:
                    ag_copy(buf, 3, d, s, b).start()

    def ag_third(buf):
        for b in everyb:
            for d, s in sides:
                ag_copy(buf, 1, d, s, b).wait_recv()
                ag_copy(buf, 2, d, s, b).start()

    def ag_fourth(buf):
        for b in everyb:
            for d, s in sides:
                ag_copy(buf, 2, d, s, b).wait_recv()
                ag_copy(buf, 3, d, s, b).start()

    def ag_last(buf, b):
        for d, s in sides:
            ag_copy(buf, 3, d, s, b).wait_recv()
            if buf != 0:
                ag_copy(buf, 2, d, s, b).wait_recv()

    def plane_copy(tick, j):
        return remote(sqp.at[tick, me_p], sqp.at[tick, me_p], pp_s.at[tick, j], pp_r.at[tick, j], pdev(j))

    def norm_first(tick, tile):
        sqp[tick, me_p] = tile
        for j in range(1, np_):
            plane_copy(tick, j).start()

    def z_copy(tick, j):
        return remote(sqs.at[tick], sqz.at[tick, z], zz_s.at[tick, j], zz_r.at[tick, j], zdev(j))

    def zo_copy(j):
        return remote(sqs.at[0], sqo.at[z], zo_s.at[j], zo_r.at[j], odev(j))

    def norm_second(tick):
        for j in range(1, np_):
            plane_copy(tick, j).wait_recv()
        total = sqp[tick, 0]
        for j in range(1, np_):
            total = total + sqp[tick, j]
        sqs[tick] = total
        sqz[tick, z] = total
        for j in range(1, nz):
            z_copy(tick, j).start()
        if tick == 0:
            @pl.when(c == 0)
            def _():
                for j in range(nz):
                    zo_copy(j).start()

    def scale_of(ref):
        total = ref[0]
        for j in range(1, nz):
            total = total + ref[j]
        sq = jnp.sum(jnp.sum(total, axis=1, keepdims=True), axis=0, keepdims=True)
        return 0.5 * jnp.sqrt(jnp.float32(3 * df * heads_all)) / jnp.sqrt(sq + 1e-06)

    def renorm(old, buf, scale, new, b):
        cols = slice(b * LANES, (b + 1) * LANES)
        for m in range(3):
            older = old[m, :, cols].astype(F32)
            moved = older + scale * gg[buf, b, m].astype(F32)
            was = jnp.sum(older * older, axis=0, keepdims=True)
            now = jnp.sum(moved * moved, axis=0, keepdims=True)
            factor = jnp.sqrt(was) / jnp.sqrt(now + 1e-06)
            new[m, :, cols] = (moved * factor).astype(BF16)

    def mix(tick, part, state, g):
        cols = slice(g * GROUP, (g + 1) * GROUP)
        q = qs[tick, part]
        p1 = jnp.dot(q, state[0, :, cols], preferred_element_type=F32)
        p3 = jnp.dot(q, state[1, :, cols], preferred_element_type=F32)
        pa[part, :, cols] = (p1 * sigmoid(p1) * p3).astype(BF16)

    tiles = tok // GROUP

    def mate_out(tick, i):
        at = pl.ds(i * GROUP, GROUP)
        return remote(os_.at[tick, at], out.at[tick, 0, core, at], os_s.at[tick, i], os_r.at[tick, i], mate)

    def apply_mate(tick, state):
        for i in range(tiles):
            at = slice(i * GROUP, (i + 1) * GROUP)
            o = lax.dot_general(pa[1, at], state[2], NT, preferred_element_type=F32)
            os_[tick, at, :] = o.astype(BF16)
            mate_out(tick, i).start()

    def apply_own(tick, state):
        o = lax.dot_general(pa[0], state[2], NT, preferred_element_type=F32)
        out[tick, 0, core] = o.astype(BF16)

    prepare(k0.at[0], v0.at[0], rate_columns(rt, 0, core), kt0, rv0, rvt0, tok)
    for g in range(ng):
        forward(k0.at[0], rv0, s0.at[0], tok, g)
        for m in order:
            part = grad(m, kt0, rvt0, tok, 2 * tok, g).astype(BF16).astype(F32)
            if m == order[0]:
                gx_copies[g].wait_recv()
            for b in blocks(g):
                gb[0, b, m] = (part[:, lanes(b)] + gxr[b, m].astype(F32)).astype(BF16)
        for b in blocks(g):
            rs_first(0, b)
        for b in blocks(g):
            rs_far(0, b)
    for cp in mate_copies:
        cp.start()
    loads[7].wait()
    loads[8].wait()
    prepare(k1.at[0], v1.at[0], rate_columns(rt, 1, core), kt1, rv1, rvt1, 0)
    for b in everyb:
        rs_second(0, b)
    for i in (0, 1, 2):
        mate_copies[i].wait_recv()
    prepare(k1.at[1], v1.at[1], rate_columns(rtp, 1, core), kt1, rv1, rvt1, tok)
    for b in everyb:
        rs_third(0, b)

    def hand_over(b):
        part = (b,) + chunk(0)
        return remote(gg.at[(0,) + part], gg.at[(1,) + part], ho_s.at[b], ho_r.at[b], twin)

    tile = jnp.zeros((8, 128), F32)
    for b in everyb:
        tile = tile + rs_last(0, b, 0)

        @pl.when(c == 0)
        def _():
            hand_over(b).start()

        ag_first(0, b)
    norm_first(0, tile)

    @pl.when(c == 0)
    def _():
        state_copies[order[2]].start()
        ag_second(0)

    @pl.when(c == 1)
    def _():
        for b in everyb:
            hand_over(b).wait_recv()
            ag_first(1, b)

    norm_second(0)

    @pl.when(c == 1)
    def _():
        ag_second(1)
        ag_third(1)
        for j in range(nz):
            zo_copy(j).wait_recv()
        for m in order:
            state_copies[m].wait_recv()

    @pl.when(c == 0)
    def _():
        fresh_load.wait()

    for g in range(ng):
        @pl.when(c == 1)
        def _():
            for b in blocks(g):
                ag_last(1, b)
            if g == 0:
                ag_second(0)
            scale = scale_of(sqo)
            for b in blocks(g):
                renorm(so, 1, scale, s2, b)

        forward(k1.at[0], rv1, s2, 0, g)
        forward(k1.at[1], rv1, s2, tok, g)
        for m in order:
            part = grad(m, kt1, rvt1, 0, 2 * tok, g).astype(BF16)
            for b in blocks(g):
                gb[1, b, m] = part[:, lanes(b)]
        for b in blocks(g):
            rs_first(1, b)
        for b in blocks(g):
            rs_far(1, b)
    for b in everyb:
        rs_second(1, b)
    for b in everyb:
        rs_third(1, b)
    ag_third(0)
    tile = jnp.zeros((8, 128), F32)
    for b in everyb:
        tile = tile + rs_last(1, b, 2)
        ag_first(2, b)
    norm_first(1, tile)
    ag_second(2)
    norm_second(1)
    ag_fourth(0)
    ag_third(2)
    for j in range(1, nz):
        z_copy(0, j).wait_recv()
    loads[9].wait()
    mate_copies[3].wait_recv()
    scale = scale_of(sqz.at[0])
    for b in everyb:
        ag_last(0, b)
        renorm(s0.at[0], 0, scale, s1, b)
    for g in range(ng):
        for part in (0, 1):
            mix(0, part, s1, g)
    apply_mate(0, s1)
    apply_own(0, s1)
    loads[10].wait()
    mate_copies[4].wait_recv()
    for j in range(1, nz):
        z_copy(1, j).wait_recv()
    scale = scale_of(sqz.at[1])
    for g in range(ng):
        for b in blocks(g):
            ag_last(2, b)
            renorm(s2, 2, scale, s3, b)
        for part in (1, 0):
            mix(1, part, s3, g)
    apply_mate(1, s3)
    apply_own(1, s3)

    for cp in gx_copies + mate_copies:
        cp.wait_send()
    for b in everyb:
        for tick in (0, 1):
            for hop in range(4):
                for d, s in sides:
                    rs_copy(tick, hop, d, s, b).wait_send()
        for buf in (0, 2):
            for hop in range(4):
                for d, s in sides:
                    ag_copy(buf, hop, d, s, b).wait_send()
    for tick in (0, 1):
        for j in range(1, np_):
            plane_copy(tick, j).wait_send()
        for j in range(1, nz):
            z_copy(tick, j).wait_send()

    @pl.when(c == 0)
    def _():
        for m in order:
            state_copies[m].wait_send()
        for b in everyb:
            hand_over(b).wait_send()
        for j in range(nz):
            zo_copy(j).wait_send()

    @pl.when(c == 1)
    def _():
        for b in everyb:
            for hop in range(4):
                for d, s in sides:
                    ag_copy(1, hop, d, s, b).wait_send()

    for tick in (0, 1):
        for i in range(tiles):
            mate_out(tick, i).wait()


def shards(mesh_shape, keys, values, queries, rates, state_in, fresh):
    nz, nh = mesh_shape["tok"] // 2, mesh_shape["head"]
    _, _, _, tok, dh = keys.shape
    df = state_in.shape[-1]
    heads_all = 2 * nh
    rows, nb = dh // nz, df // LANES
    cut = (nb, 3, dh, LANES)
    sizes = (nz, nh, tok, dh, df, heads_all)
    dma = pltpu.SemaphoreType.DMA

    def vm(*shape, dtype=BF16):
        return pltpu.VMEM(shape, dtype)

    both = 2 * tok
    state = (3, dh, df)
    scratch = [
        vm(2, tok, dh), vm(2, tok, dh), vm(2, tok, dh), vm(2, tok, dh), vm(2, 2, tok, dh), vm(2, tok, dh),
        vm(*rates.shape, dtype=F32), vm(*rates.shape, dtype=F32),
        vm(2, *state), vm(*state), vm(*state), vm(*state), vm(*state),
        vm(dh, both), vm(both, dh), vm(dh, both), vm(dh, both), vm(both, dh), vm(dh, both),
        vm(both, df), vm(both, df), vm(both, df), vm(2, tok, df),
        vm(*cut), vm(*cut), vm(2, *cut), vm(3, *cut),
        vm(2, 3, 2, nb, 3, rows, LANES), vm(2, 2, nb, 3, rows // 2, LANES), vm(2, 2, 2, nb, 3, rows, LANES),
        vm(2, 2 * nh, 8, 128, dtype=F32), vm(2, 8, 128, dtype=F32), vm(2, nz, 8, 128, dtype=F32), vm(nz, 8, 128, dtype=F32),
        dma((12,)), dma((5,)), dma((5,)), dma((3,)), dma((3,)),
        dma((2, 4, 2, nb)), dma((2, 4, 2, nb)), dma((3, 4, 2, nb)), dma((3, 4, 2, nb)),
        dma((nb,)), dma((nb,)), dma((3,)), dma((3,)),
        dma((2, 2 * nh)), dma((2, 2 * nh)), dma((2, nz)), dma((2, nz)), dma((nz,)), dma((nz,)),
        dma((2, tok // GROUP)), dma((2, tok // GROUP)),
    ]
    return pl.pallas_call(
        functools.partial(kernel, sizes),
        out_shape=pltpu.VMEM(queries.shape, BF16),
        in_specs=[pl.BlockSpec(memory_space=pltpu.HBM)] * 6,
        out_specs=pl.BlockSpec(memory_space=pltpu.VMEM),
        scratch_shapes=scratch,
        compiler_params=pltpu.CompilerParams(
            collective_id=0, has_side_effects=True, vmem_limit_bytes=40 * 1024 * 1024
        ),
        cost_estimate=pl.CostEstimate(flops=8_000_000_000, bytes_accessed=10_000_000, transcendentals=3_000_000),
    )(*(pltpu.with_memory_space_constraint(a, pltpu.HBM) for a in (keys, values, queries, rates, state_in, fresh)))


def solution(mesh):
    in_specs = (
        P(None, "ctx", "head", "tok", None),
        P(None, "ctx", "head", "tok", None),
        P(None, "ctx", "head", "tok", None),
        P(None, "ctx", "head", "tok"),
        P("ctx", "head", None, None, None),
        P("head", None, None, None),
    )
    return jax.shard_map(
        functools.partial(shards, dict(mesh.shape)),
        mesh=mesh,
        in_specs=in_specs,
        out_specs=P(None, "ctx", "head", "tok", None),
        check_vma=False,
    )
```

```python
import functools

import jax
import jax.numpy as jnp
from jax import lax
from jax.experimental import pallas as pl
from jax.experimental.pallas import tpu as pltpu
from jax.sharding import PartitionSpec as P

MESH = pl.DeviceIdType.MESH
F32, BF16 = jnp.float32, jnp.bfloat16
LANES, GROUP = 128, 256
NT = (((1,), (1,)), ((), ()))


def sigmoid(x):
    return 0.5 * jnp.tanh(0.5 * x) + 0.5


def kernel(
    sizes,
    keys, values, queries, rates, state_in, fresh,
    out,
    k0, v0, k1, v1, qs, os_, rt, rtp, s0, so, s1, s2, s3,
    kt0, rv0, rvt0, kt1, rv1, rvt1, act, d1, d3, pa,
    gx, gxr, gb, gg, rin, rhalf, rout,
    sqp, sqs, sqz, sqo,
    load_sem, xs, xr, gxs, gxrs, rs_s, rs_r, ag_s, ag_r, ho_s, ho_r, st_s, st_r,
    pp_s, pp_r, zz_s, zz_r, zo_s, zo_r, os_s, os_r,
):
    nz, nh, tok, dh, df, heads_all = sizes
    rows = dh // nz
    half = rows // 2
    nb, ng = df // LANES, df // GROUP
    per = nb // ng
    c, t, h = lax.axis_index("ctx"), lax.axis_index("tok"), lax.axis_index("head")
    z, core = t // 2, t % 2
    other = 1 - core
    np_ = 2 * nh
    me_p = h * 2 + core

    def zdev(step):
        return (c, lax.rem(z + step + nz, nz) * 2 + core, h)

    def pdev(j):
        p = lax.rem(me_p + j, np_)
        return (c, z * 2 + lax.rem(p, 2), p // 2)

    def odev(step):
        return (1 - c, lax.rem(z + step, nz) * 2 + core, h)

    mate = (c, z * 2 + other, h)
    twin = (1 - c, t, h)

    local = [
        (keys.at[0, 0, other], k0.at[1]),
        (state_in.at[0, other], s0.at[1]),
        (values.at[0, 0, other], v0.at[1]),
        (rates, rt),
        (keys.at[0, 0, core], k0.at[0]),
        (state_in.at[0, core], s0.at[0]),
        (values.at[0, 0, core], v0.at[0]),
        (keys.at[1, 0, core], k1.at[0]),
        (values.at[1, 0, core], v1.at[0]),
        (queries.at[0, 0, core], qs.at[0, 0]),
        (queries.at[1, 0, core], qs.at[1, 0]),
    ]
    loads = [pltpu.make_async_copy(a, b, load_sem.at[i]) for i, (a, b) in enumerate(local)]
    for i in (0, 1, 2, 3):
        loads[i].start()
    fresh_load = pltpu.make_async_copy(fresh.at[core], s2, load_sem.at[len(local)])

    barrier = pltpu.get_barrier_semaphore()
    for j in range(1, np_):
        pl.semaphore_signal(barrier, inc=1, device_id=pdev(j), device_id_type=MESH)
    for j in range(1, nz):
        pl.semaphore_signal(barrier, inc=1, device_id=zdev(j), device_id_type=MESH)
    for j in range(nz):
        pl.semaphore_signal(barrier, inc=1, device_id=odev(j), device_id_type=MESH)

    def remote(src, dst, ss, rs, dev):
        return pltpu.make_async_remote_copy(
            src_ref=src, dst_ref=dst, send_sem=ss, recv_sem=rs, device_id=dev, device_id_type=MESH
        )

    def rate_columns(ref, tick, head):
        row = jnp.where(head == 0, ref[tick, 0, 0:1, :], ref[tick, 0, 1:2, :])
        col = jnp.broadcast_to(row, (128, tok)).T
        return jnp.concatenate([col] * (dh // 128), axis=1)

    def prepare(k, v, col, kt, rv, rvt, lo):
        kt[:, lo:lo + tok] = k[...].T
        weighted = (v[...].astype(F32) * col).astype(BF16)
        rv[lo:lo + tok, :] = weighted
        rvt[:, lo:lo + tok] = weighted.T

    def forward(k, rv, state, lo, g):
        at, cols = slice(lo, lo + tok), slice(g * GROUP, (g + 1) * GROUP)
        kk = k[...]
        h1 = jnp.dot(kk, state[0, :, cols], preferred_element_type=F32)
        h3 = jnp.dot(kk, state[1, :, cols], preferred_element_type=F32)
        dact = jnp.dot(rv[at, :], state[2, :, cols], preferred_element_type=F32)
        sig = sigmoid(h1)
        hs = h1 * sig
        act[at, cols] = (hs * h3).astype(BF16)
        d3[at, cols] = (dact * hs).astype(BF16)
        d1[at, cols] = (dact * h3 * (sig + hs * (1.0 - sig))).astype(BF16)

    def grad(m, kt, rvt, lo, hi, g):
        left, right = ((kt, d1), (kt, d3), (rvt, act))[m]
        cols = slice(g * GROUP, (g + 1) * GROUP)
        return jnp.dot(left[:, lo:hi], right[lo:hi, cols], preferred_element_type=F32)

    def blocks(g):
        return range(g * per, (g + 1) * per)

    def lanes(b):
        return slice((b % per) * LANES, (b % per + 1) * LANES)

    order = (2, 0, 1)
    everyb = tuple(range(nb))

    for i in (4, 5, 6):
        loads[i].start()
    for i in (0, 1, 2, 3):
        loads[i].wait()
    prepare(k0.at[1], v0.at[1], rate_columns(rt, 0, other), kt0, rv0, rvt0, 0)
    for i in (7, 8, 9, 10):
        loads[i].start()

    @pl.when(c == 0)
    def _():
        fresh_load.start()

    for g in range(ng):
        forward(k0.at[1], rv0, s0.at[1], 0, g)
        for m in order:
            part = grad(m, kt0, rvt0, 0, tok, g).astype(BF16)
            for b in blocks(g):
                gx[b, m] = part[:, lanes(b)]

    pl.semaphore_wait(barrier, np_ - 1 + nz - 1 + nz)

    gx_copies = [
        remote(gx.at[pl.ds(g * per, per)], gxr.at[pl.ds(g * per, per)], gxs.at[g], gxrs.at[g], mate) for g in range(ng)
    ]
    for cp in gx_copies:
        cp.start()
    state_copies = {m: remote(s0.at[0, m], so.at[m], st_s.at[m], st_r.at[m], twin) for m in order}
    for i in (4, 5, 6):
        loads[i].wait()

    @pl.when(c == 0)
    def _():
        state_copies[order[0]].start()
        state_copies[order[1]].start()

    mate_copies = [
        remote(src, dst, xs.at[i], xr.at[i], mate)
        for i, (src, dst) in enumerate([
            (rates, rtp),
            (keys.at[1, 0, other], k1.at[1]),
            (values.at[1, 0, other], v1.at[1]),
            (queries.at[0, 0, other], qs.at[0, 1]),
            (queries.at[1, 0, other], qs.at[1, 1]),
        ])
    ]

    def chunk(owner_step, part=None):
        owner = lax.rem(z + owner_step + 2 * nz, nz)
        if part is None:
            return (slice(None), pl.ds(pl.multiple_of(owner * rows, rows), rows), slice(None))
        return (slice(None), pl.ds(pl.multiple_of(owner * rows + part * half, half), half), slice(None))

    sides = ((0, -1), (1, 1))

    def rs_copy(tick, hop, d, s, b):
        if hop == 0:
            src, dst, dev = gb.at[(tick, b) + chunk(3 * s)], rin.at[tick, 0, d, b], zdev(s)
        elif hop == 1:
            src, dst, dev = gb.at[(tick, b) + chunk(4, d)], rhalf.at[tick, d, b], zdev(3 * s)
        else:
            src, dst, dev = rout.at[tick, hop - 2, d, b], rin.at[tick, hop - 1, d, b], zdev(s)
        return remote(src, dst, rs_s.at[tick, hop, d, b], rs_r.at[tick, hop, d, b], dev)

    def rs_first(tick, b):
        for d, s in sides:
            rs_copy(tick, 0, d, s, b).start()

    def rs_far(tick, b):
        for d, s in sides:
            rs_copy(tick, 1, d, s, b).start()

    def rs_second(tick, b):
        for d, s in sides:
            rs_copy(tick, 0, d, s, b).wait_recv()
            own = gb[(tick, b) + chunk(2 * s)].astype(F32) + rin[tick, 0, d, b].astype(F32)
            rout[tick, 0, d, b] = own.astype(BF16)
            rs_copy(tick, 2, d, s, b).start()

    def rs_third(tick, b):
        for d, s in sides:
            rs_copy(tick, 2, d, s, b).wait_recv()
            rs_copy(tick, 1, d, s, b).wait_recv()
            own = gb[(tick, b) + chunk(s)].astype(F32) + rin[tick, 1, d, b].astype(F32)
            far = rhalf[tick, d, b].astype(F32)
            if d == 0:
                rout[tick, 1, d, b, :, 0:half, :] = (own[:, 0:half] + far).astype(BF16)
                rout[tick, 1, d, b, :, half:rows, :] = own[:, half:rows].astype(BF16)
            else:
                rout[tick, 1, d, b, :, 0:half, :] = own[:, 0:half].astype(BF16)
                rout[tick, 1, d, b, :, half:rows, :] = (own[:, half:rows] + far).astype(BF16)
            rs_copy(tick, 3, d, s, b).start()

    def rs_last(tick, b, buf):
        total = gb[(tick, b) + chunk(0)].astype(F32)
        for d, s in sides:
            rs_copy(tick, 3, d, s, b).wait_recv()
            total = total + rin[tick, 2, d, b].astype(F32)
        gg[(buf, b) + chunk(0)] = total.astype(BF16)
        square = total * total
        tile = jnp.zeros((8, 128), F32)
        for m in range(3):
            for i in range(0, rows, 8):
                tile = tile + square[m, i:i + 8]
        return tile

    def ag_copy(buf, hop, d, s, b):
        if hop == 0:
            part, dev = chunk(0), zdev(s)
        elif hop == 1:
            part, dev = chunk(-s), zdev(s)
        elif hop == 2:
            part, dev = chunk(-2 * s), zdev(s)
        elif buf == 0:
            part, dev = chunk(-3 * s, d), zdev(s)
        else:
            part, dev = chunk(-s, d), zdev(3 * s)
        part = (buf, b) + part
        return remote(gg.at[part], gg.at[part], ag_s.at[buf, hop, d, b], ag_r.at[buf, hop, d, b], dev)

    def ag_first(buf, b):
        for d, s in sides:
            ag_copy(buf, 0, d, s, b).start()

    def ag_second(buf):
        for b in everyb:
            for d, s in sides:
                ag_copy(buf, 0, d, s, b).wait_recv()
                ag_copy(buf, 1, d, s, b).start()
        if buf != 0:
            for b in everyb:
                for d, s in sides:
                    ag_copy(buf, 3, d, s, b).start()

    def ag_third(buf):
        for b in everyb:
            for d, s in sides:
                ag_copy(buf, 1, d, s, b).wait_recv()
                ag_copy(buf, 2, d, s, b).start()

    def ag_fourth(buf):
        for b in everyb:
            for d, s in sides:
                ag_copy(buf, 2, d, s, b).wait_recv()
                ag_copy(buf, 3, d, s, b).start()

    def ag_last(buf, b):
        for d, s in sides:
            ag_copy(buf, 3, d, s, b).wait_recv()
            if buf != 0:
                ag_copy(buf, 2, d, s, b).wait_recv()

    def plane_copy(tick, j):
        return remote(sqp.at[tick, me_p], sqp.at[tick, me_p], pp_s.at[tick, j], pp_r.at[tick, j], pdev(j))

    def norm_first(tick, tile):
        sqp[tick, me_p] = tile
        for j in range(1, np_):
            plane_copy(tick, j).start()

    def z_copy(tick, j):
        return remote(sqs.at[tick], sqz.at[tick, z], zz_s.at[tick, j], zz_r.at[tick, j], zdev(j))

    def zo_copy(j):
        return remote(sqs.at[0], sqo.at[z], zo_s.at[j], zo_r.at[j], odev(j))

    def norm_second(tick):
        for j in range(1, np_):
            plane_copy(tick, j).wait_recv()
        total = sqp[tick, 0]
        for j in range(1, np_):
            total = total + sqp[tick, j]
        sqs[tick] = total
        sqz[tick, z] = total
        for j in range(1, nz):
            z_copy(tick, j).start()
        if tick == 0:
            @pl.when(c == 0)
            def _():
                for j in range(nz):
                    zo_copy(j).start()

    def scale_of(ref):
        total = ref[0]
        for j in range(1, nz):
            total = total + ref[j]
        sq = jnp.sum(jnp.sum(total, axis=1, keepdims=True), axis=0, keepdims=True)
        return 0.5 * jnp.sqrt(jnp.float32(3 * df * heads_all)) / jnp.sqrt(sq + 1e-06)

    def renorm(old, buf, scale, new, b):
        cols = slice(b * LANES, (b + 1) * LANES)
        for m in range(3):
            older = old[m, :, cols].astype(F32)
            moved = older + scale * gg[buf, b, m].astype(F32)
            was = jnp.sum(older * older, axis=0, keepdims=True)
            now = jnp.sum(moved * moved, axis=0, keepdims=True)
            factor = jnp.sqrt(was) / jnp.sqrt(now + 1e-06)
            new[m, :, cols] = (moved * factor).astype(BF16)

    def mix(tick, part, state, g):
        cols = slice(g * GROUP, (g + 1) * GROUP)
        q = qs[tick, part]
        p1 = jnp.dot(q, state[0, :, cols], preferred_element_type=F32)
        p3 = jnp.dot(q, state[1, :, cols], preferred_element_type=F32)
        pa[part, :, cols] = (p1 * sigmoid(p1) * p3).astype(BF16)

    tiles = tok // GROUP

    def mate_out(tick, i):
        at = pl.ds(i * GROUP, GROUP)
        return remote(os_.at[tick, at], out.at[tick, 0, core, at], os_s.at[tick, i], os_r.at[tick, i], mate)

    def apply_mate(tick, state):
        for i in range(tiles):
            at = slice(i * GROUP, (i + 1) * GROUP)
            o = lax.dot_general(pa[1, at], state[2], NT, preferred_element_type=F32)
            os_[tick, at, :] = o.astype(BF16)
            mate_out(tick, i).start()

    def apply_own(tick, state):
        o = lax.dot_general(pa[0], state[2], NT, preferred_element_type=F32)
        out[tick, 0, core] = o.astype(BF16)

    prepare(k0.at[0], v0.at[0], rate_columns(rt, 0, core), kt0, rv0, rvt0, tok)
    for g in range(ng):
        forward(k0.at[0], rv0, s0.at[0], tok, g)
        for m in order:
            part = grad(m, kt0, rvt0, tok, 2 * tok, g).astype(BF16).astype(F32)
            if m == order[0]:
                gx_copies[g].wait_recv()
            for b in blocks(g):
                gb[0, b, m] = (part[:, lanes(b)] + gxr[b, m].astype(F32)).astype(BF16)
        for b in blocks(g):
            rs_first(0, b)
        for b in blocks(g):
            rs_far(0, b)
    for cp in mate_copies:
        cp.start()
    loads[7].wait()
    loads[8].wait()
    prepare(k1.at[0], v1.at[0], rate_columns(rt, 1, core), kt1, rv1, rvt1, 0)
    for b in everyb:
        rs_second(0, b)
    for i in (0, 1, 2):
        mate_copies[i].wait_recv()
    prepare(k1.at[1], v1.at[1], rate_columns(rtp, 1, core), kt1, rv1, rvt1, tok)
    for b in everyb:
        rs_third(0, b)

    def hand_over(b):
        part = (b,) + chunk(0)
        return remote(gg.at[(0,) + part], gg.at[(1,) + part], ho_s.at[b], ho_r.at[b], twin)

    tile = jnp.zeros((8, 128), F32)
    for b in everyb:
        tile = tile + rs_last(0, b, 0)

        @pl.when(c == 0)
        def _():
            hand_over(b).start()

        ag_first(0, b)
    norm_first(0, tile)

    @pl.when(c == 0)
    def _():
        state_copies[order[2]].start()
        ag_second(0)

    @pl.when(c == 1)
    def _():
        for b in everyb:
            hand_over(b).wait_recv()
            ag_first(1, b)

    norm_second(0)

    @pl.when(c == 1)
    def _():
        ag_second(1)
        ag_third(1)
        for j in range(nz):
            zo_copy(j).wait_recv()
        for m in order:
            state_copies[m].wait_recv()

    @pl.when(c == 0)
    def _():
        fresh_load.wait()

    for g in range(ng):
        @pl.when(c == 1)
        def _():
            for b in blocks(g):
                ag_last(1, b)
            if g == 0:
                ag_second(0)
            scale = scale_of(sqo)
            for b in blocks(g):
                renorm(so, 1, scale, s2, b)

        forward(k1.at[0], rv1, s2, 0, g)
        forward(k1.at[1], rv1, s2, tok, g)
        for m in order:
            part = grad(m, kt1, rvt1, 0, 2 * tok, g).astype(BF16)
            for b in blocks(g):
                gb[1, b, m] = part[:, lanes(b)]
        for b in blocks(g):
            rs_first(1, b)
        for b in blocks(g):
            rs_far(1, b)
    for b in everyb:
        rs_second(1, b)
    ag_third(0)
    for b in everyb:
        rs_third(1, b)
    ag_fourth(0)
    tile = jnp.zeros((8, 128), F32)
    for b in everyb:
        tile = tile + rs_last(1, b, 2)
        ag_first(2, b)
    norm_first(1, tile)
    for j in range(1, nz):
        z_copy(0, j).wait_recv()
    loads[9].wait()
    mate_copies[3].wait_recv()
    scale = scale_of(sqz.at[0])
    for b in everyb:
        ag_last(0, b)
        renorm(s0.at[0], 0, scale, s1, b)
    for part in (0, 1):
        mix(0, part, s1, 0)
    ag_second(2)
    norm_second(1)
    for g in range(1, ng):
        for part in (0, 1):
            mix(0, part, s1, g)
    apply_mate(0, s1)
    ag_third(2)
    apply_own(0, s1)
    loads[10].wait()
    mate_copies[4].wait_recv()
    for j in range(1, nz):
        z_copy(1, j).wait_recv()
    scale = scale_of(sqz.at[1])
    for g in range(ng):
        for b in blocks(g):
            ag_last(2, b)
            renorm(s2, 2, scale, s3, b)
        for part in (1, 0):
            mix(1, part, s3, g)
    apply_mate(1, s3)
    apply_own(1, s3)

    for cp in gx_copies + mate_copies:
        cp.wait_send()
    for b in everyb:
        for tick in (0, 1):
            for hop in range(4):
                for d, s in sides:
                    rs_copy(tick, hop, d, s, b).wait_send()
        for buf in (0, 2):
            for hop in range(4):
                for d, s in sides:
                    ag_copy(buf, hop, d, s, b).wait_send()
    for tick in (0, 1):
        for j in range(1, np_):
            plane_copy(tick, j).wait_send()
        for j in range(1, nz):
            z_copy(tick, j).wait_send()

    @pl.when(c == 0)
    def _():
        for m in order:
            state_copies[m].wait_send()
        for b in everyb:
            hand_over(b).wait_send()
        for j in range(nz):
            zo_copy(j).wait_send()

    @pl.when(c == 1)
    def _():
        for b in everyb:
            for hop in range(4):
                for d, s in sides:
                    ag_copy(1, hop, d, s, b).wait_send()

    for tick in (0, 1):
        for i in range(tiles):
            mate_out(tick, i).wait()


def shards(mesh_shape, keys, values, queries, rates, state_in, fresh):
    nz, nh = mesh_shape["tok"] // 2, mesh_shape["head"]
    _, _, _, tok, dh = keys.shape
    df = state_in.shape[-1]
    heads_all = 2 * nh
    rows, nb = dh // nz, df // LANES
    cut = (nb, 3, dh, LANES)
    sizes = (nz, nh, tok, dh, df, heads_all)
    dma = pltpu.SemaphoreType.DMA

    def vm(*shape, dtype=BF16):
        return pltpu.VMEM(shape, dtype)

    both = 2 * tok
    state = (3, dh, df)
    scratch = [
        vm(2, tok, dh), vm(2, tok, dh), vm(2, tok, dh), vm(2, tok, dh), vm(2, 2, tok, dh), vm(2, tok, dh),
        vm(*rates.shape, dtype=F32), vm(*rates.shape, dtype=F32),
        vm(2, *state), vm(*state), vm(*state), vm(*state), vm(*state),
        vm(dh, both), vm(both, dh), vm(dh, both), vm(dh, both), vm(both, dh), vm(dh, both),
        vm(both, df), vm(both, df), vm(both, df), vm(2, tok, df),
        vm(*cut), vm(*cut), vm(2, *cut), vm(3, *cut),
        vm(2, 3, 2, nb, 3, rows, LANES), vm(2, 2, nb, 3, rows // 2, LANES), vm(2, 2, 2, nb, 3, rows, LANES),
        vm(2, 2 * nh, 8, 128, dtype=F32), vm(2, 8, 128, dtype=F32), vm(2, nz, 8, 128, dtype=F32), vm(nz, 8, 128, dtype=F32),
        dma((12,)), dma((5,)), dma((5,)), dma((3,)), dma((3,)),
        dma((2, 4, 2, nb)), dma((2, 4, 2, nb)), dma((3, 4, 2, nb)), dma((3, 4, 2, nb)),
        dma((nb,)), dma((nb,)), dma((3,)), dma((3,)),
        dma((2, 2 * nh)), dma((2, 2 * nh)), dma((2, nz)), dma((2, nz)), dma((nz,)), dma((nz,)),
        dma((2, tok // GROUP)), dma((2, tok // GROUP)),
    ]
    return pl.pallas_call(
        functools.partial(kernel, sizes),
        out_shape=pltpu.VMEM(queries.shape, BF16),
        in_specs=[pl.BlockSpec(memory_space=pltpu.HBM)] * 6,
        out_specs=pl.BlockSpec(memory_space=pltpu.VMEM),
        scratch_shapes=scratch,
        compiler_params=pltpu.CompilerParams(
            collective_id=0, has_side_effects=True, vmem_limit_bytes=40 * 1024 * 1024
        ),
        cost_estimate=pl.CostEstimate(flops=8_000_000_000, bytes_accessed=10_000_000, transcendentals=3_000_000),
    )(*(pltpu.with_memory_space_constraint(a, pltpu.HBM) for a in (keys, values, queries, rates, state_in, fresh)))


def solution(mesh):
    in_specs = (
        P(None, "ctx", "head", "tok", None),
        P(None, "ctx", "head", "tok", None),
        P(None, "ctx", "head", "tok", None),
        P(None, "ctx", "head", "tok"),
        P("ctx", "head", None, None, None),
        P("head", None, None, None),
    )
    return jax.shard_map(
        functools.partial(shards, dict(mesh.shape)),
        mesh=mesh,
        in_specs=in_specs,
        out_specs=P(None, "ctx", "head", "tok", None),
        check_vma=False,
    )
```

```python
import functools

import jax
import jax.numpy as jnp
from jax import lax
from jax.experimental import pallas as pl
from jax.experimental.pallas import tpu as pltpu
from jax.sharding import PartitionSpec as P

MESH = pl.DeviceIdType.MESH
F32, BF16 = jnp.float32, jnp.bfloat16
LANES, GROUP = 128, 256
NT = (((1,), (1,)), ((), ()))


def sigmoid(x):
    return 0.5 * jnp.tanh(0.5 * x) + 0.5


def kernel(
    sizes,
    keys, values, queries, rates, state_in, fresh,
    out,
    k0, v0, k1, v1, qs, os_, rt, rtp, s0, so, s1, s2, s3,
    kt0, rv0, rvt0, kt1, rv1, rvt1, act, d1, d3, pa,
    gx, gxr, gb, gg, rin, rhalf, rout,
    sqp, sqs, sqz, sqo,
    load_sem, xs, xr, gxs, gxrs, rs_s, rs_r, ag_s, ag_r, ho_s, ho_r, st_s, st_r,
    pp_s, pp_r, zz_s, zz_r, zo_s, zo_r, os_s, os_r,
):
    nz, nh, tok, dh, df, heads_all = sizes
    rows = dh // nz
    half = rows // 2
    nb, ng = df // LANES, df // GROUP
    per = nb // ng
    c, t, h = lax.axis_index("ctx"), lax.axis_index("tok"), lax.axis_index("head")
    z, core = t // 2, t % 2
    other = 1 - core
    np_ = 2 * nh
    me_p = h * 2 + core

    def zdev(step):
        return (c, lax.rem(z + step + nz, nz) * 2 + core, h)

    def pdev(j):
        p = lax.rem(me_p + j, np_)
        return (c, z * 2 + lax.rem(p, 2), p // 2)

    def odev(step):
        return (1 - c, lax.rem(z + step, nz) * 2 + core, h)

    mate = (c, z * 2 + other, h)
    twin = (1 - c, t, h)

    local = [
        (keys.at[0, 0, other], k0.at[1]),
        (state_in.at[0, other], s0.at[1]),
        (values.at[0, 0, other], v0.at[1]),
        (rates, rt),
        (keys.at[0, 0, core], k0.at[0]),
        (state_in.at[0, core], s0.at[0]),
        (values.at[0, 0, core], v0.at[0]),
        (keys.at[1, 0, core], k1.at[0]),
        (values.at[1, 0, core], v1.at[0]),
        (queries.at[0, 0, core], qs.at[0, 0]),
        (queries.at[1, 0, core], qs.at[1, 0]),
    ]
    loads = [pltpu.make_async_copy(a, b, load_sem.at[i]) for i, (a, b) in enumerate(local)]
    for i in (0, 1, 2, 3):
        loads[i].start()
    fresh_load = pltpu.make_async_copy(fresh.at[core], s2, load_sem.at[len(local)])

    barrier = pltpu.get_barrier_semaphore()
    for j in range(1, np_):
        pl.semaphore_signal(barrier, inc=1, device_id=pdev(j), device_id_type=MESH)
    for j in range(1, nz):
        pl.semaphore_signal(barrier, inc=1, device_id=zdev(j), device_id_type=MESH)
    for j in range(nz):
        pl.semaphore_signal(barrier, inc=1, device_id=odev(j), device_id_type=MESH)

    def remote(src, dst, ss, rs, dev):
        return pltpu.make_async_remote_copy(
            src_ref=src, dst_ref=dst, send_sem=ss, recv_sem=rs, device_id=dev, device_id_type=MESH
        )

    def rate_columns(ref, tick, head):
        row = jnp.where(head == 0, ref[tick, 0, 0:1, :], ref[tick, 0, 1:2, :])
        col = jnp.broadcast_to(row, (128, tok)).T
        return jnp.concatenate([col] * (dh // 128), axis=1)

    def prepare(k, v, col, kt, rv, rvt, lo):
        kt[:, lo:lo + tok] = k[...].T
        weighted = (v[...].astype(F32) * col).astype(BF16)
        rv[lo:lo + tok, :] = weighted
        rvt[:, lo:lo + tok] = weighted.T

    def forward(k, rv, state, lo, g):
        at, cols = slice(lo, lo + tok), slice(g * GROUP, (g + 1) * GROUP)
        kk = k[...]
        h1 = jnp.dot(kk, state[0, :, cols], preferred_element_type=F32)
        h3 = jnp.dot(kk, state[1, :, cols], preferred_element_type=F32)
        dact = jnp.dot(rv[at, :], state[2, :, cols], preferred_element_type=F32)
        sig = sigmoid(h1)
        hs = h1 * sig
        act[at, cols] = (hs * h3).astype(BF16)
        d3[at, cols] = (dact * hs).astype(BF16)
        d1[at, cols] = (dact * h3 * (sig + hs * (1.0 - sig))).astype(BF16)

    def grad(m, kt, rvt, lo, hi, g):
        left, right = ((kt, d1), (kt, d3), (rvt, act))[m]
        cols = slice(g * GROUP, (g + 1) * GROUP)
        return jnp.dot(left[:, lo:hi], right[lo:hi, cols], preferred_element_type=F32)

    def blocks(g):
        return range(g * per, (g + 1) * per)

    def lanes(b):
        return slice((b % per) * LANES, (b % per + 1) * LANES)

    order = (2, 0, 1)
    everyb = tuple(range(nb))

    for i in (4, 5, 6):
        loads[i].start()
    for i in (0, 1, 2, 3):
        loads[i].wait()
    prepare(k0.at[1], v0.at[1], rate_columns(rt, 0, other), kt0, rv0, rvt0, 0)
    for i in (7, 8, 9, 10):
        loads[i].start()

    @pl.when(c == 0)
    def _():
        fresh_load.start()

    for g in range(ng):
        forward(k0.at[1], rv0, s0.at[1], 0, g)
        for m in order:
            part = grad(m, kt0, rvt0, 0, tok, g).astype(BF16)
            for b in blocks(g):
                gx[b, m] = part[:, lanes(b)]

    pl.semaphore_wait(barrier, np_ - 1 + nz - 1 + nz)

    gx_copies = [
        remote(gx.at[pl.ds(g * per, per)], gxr.at[pl.ds(g * per, per)], gxs.at[g], gxrs.at[g], mate) for g in range(ng)
    ]
    for cp in gx_copies:
        cp.start()
    state_copies = {m: remote(s0.at[0, m], so.at[m], st_s.at[m], st_r.at[m], twin) for m in order}
    for i in (4, 5, 6):
        loads[i].wait()

    @pl.when(c == 0)
    def _():
        state_copies[order[0]].start()
        state_copies[order[1]].start()

    mate_copies = [
        remote(src, dst, xs.at[i], xr.at[i], mate)
        for i, (src, dst) in enumerate([
            (rates, rtp),
            (keys.at[1, 0, other], k1.at[1]),
            (values.at[1, 0, other], v1.at[1]),
            (queries.at[0, 0, other], qs.at[0, 1]),
            (queries.at[1, 0, other], qs.at[1, 1]),
        ])
    ]

    def chunk(owner_step, part=None):
        owner = lax.rem(z + owner_step + 2 * nz, nz)
        if part is None:
            return (slice(None), pl.ds(pl.multiple_of(owner * rows, rows), rows), slice(None))
        return (slice(None), pl.ds(pl.multiple_of(owner * rows + part * half, half), half), slice(None))

    sides = ((0, -1), (1, 1))

    def rs_copy(tick, hop, d, s, b):
        if hop == 0:
            src, dst, dev = gb.at[(tick, b) + chunk(3 * s)], rin.at[tick, 0, d, b], zdev(s)
        elif hop == 1:
            src, dst, dev = gb.at[(tick, b) + chunk(4, d)], rhalf.at[tick, d, b], zdev(3 * s)
        else:
            src, dst, dev = rout.at[tick, hop - 2, d, b], rin.at[tick, hop - 1, d, b], zdev(s)
        return remote(src, dst, rs_s.at[tick, hop, d, b], rs_r.at[tick, hop, d, b], dev)

    def rs_first(tick, b):
        for d, s in sides:
            rs_copy(tick, 0, d, s, b).start()

    def rs_far(tick, b):
        for d, s in sides:
            rs_copy(tick, 1, d, s, b).start()

    def rs_second(tick, b):
        for d, s in sides:
            rs_copy(tick, 0, d, s, b).wait_recv()
            own = gb[(tick, b) + chunk(2 * s)].astype(F32) + rin[tick, 0, d, b].astype(F32)
            rout[tick, 0, d, b] = own.astype(BF16)
            rs_copy(tick, 2, d, s, b).start()

    def rs_third(tick, b):
        for d, s in sides:
            rs_copy(tick, 2, d, s, b).wait_recv()
            rs_copy(tick, 1, d, s, b).wait_recv()
            own = gb[(tick, b) + chunk(s)].astype(F32) + rin[tick, 1, d, b].astype(F32)
            far = rhalf[tick, d, b].astype(F32)
            if d == 0:
                rout[tick, 1, d, b, :, 0:half, :] = (own[:, 0:half] + far).astype(BF16)
                rout[tick, 1, d, b, :, half:rows, :] = own[:, half:rows].astype(BF16)
            else:
                rout[tick, 1, d, b, :, 0:half, :] = own[:, 0:half].astype(BF16)
                rout[tick, 1, d, b, :, half:rows, :] = (own[:, half:rows] + far).astype(BF16)
            rs_copy(tick, 3, d, s, b).start()

    def rs_last(tick, b, buf):
        total = gb[(tick, b) + chunk(0)].astype(F32)
        for d, s in sides:
            rs_copy(tick, 3, d, s, b).wait_recv()
            total = total + rin[tick, 2, d, b].astype(F32)
        gg[(buf, b) + chunk(0)] = total.astype(BF16)
        square = total * total
        tile = jnp.zeros((8, 128), F32)
        for m in range(3):
            for i in range(0, rows, 8):
                tile = tile + square[m, i:i + 8]
        return tile

    def ag_copy(buf, hop, d, s, b):
        if hop == 0:
            part, dev = chunk(0), zdev(s)
        elif hop == 1:
            part, dev = chunk(-s), zdev(s)
        elif hop == 2:
            part, dev = chunk(-2 * s), zdev(s)
        elif buf == 0:
            part, dev = chunk(-3 * s, d), zdev(s)
        else:
            part, dev = chunk(-s, d), zdev(3 * s)
        part = (buf, b) + part
        return remote(gg.at[part], gg.at[part], ag_s.at[buf, hop, d, b], ag_r.at[buf, hop, d, b], dev)

    def ag_first(buf, b):
        for d, s in sides:
            ag_copy(buf, 0, d, s, b).start()

    def ag_second(buf):
        for g in range(ng):
            for b in blocks(g):
                for d, s in sides:
                    ag_copy(buf, 0, d, s, b).wait_recv()
                    ag_copy(buf, 1, d, s, b).start()
            if buf != 0:
                for b in blocks(g):
                    for d, s in sides:
                        ag_copy(buf, 3, d, s, b).start()

    def ag_third(buf):
        for b in everyb:
            for d, s in sides:
                ag_copy(buf, 1, d, s, b).wait_recv()
                ag_copy(buf, 2, d, s, b).start()

    def ag_fourth(buf):
        for b in everyb:
            for d, s in sides:
                ag_copy(buf, 2, d, s, b).wait_recv()
                ag_copy(buf, 3, d, s, b).start()

    def ag_last(buf, b):
        for d, s in sides:
            ag_copy(buf, 3, d, s, b).wait_recv()
            if buf != 0:
                ag_copy(buf, 2, d, s, b).wait_recv()

    def plane_copy(tick, j):
        return remote(sqp.at[tick, me_p], sqp.at[tick, me_p], pp_s.at[tick, j], pp_r.at[tick, j], pdev(j))

    def norm_first(tick, tile):
        sqp[tick, me_p] = tile
        for j in range(1, np_):
            plane_copy(tick, j).start()

    def z_copy(tick, j):
        return remote(sqs.at[tick], sqz.at[tick, z], zz_s.at[tick, j], zz_r.at[tick, j], zdev(j))

    def zo_copy(j):
        return remote(sqs.at[0], sqo.at[z], zo_s.at[j], zo_r.at[j], odev(j))

    def norm_second(tick):
        for j in range(1, np_):
            plane_copy(tick, j).wait_recv()
        total = sqp[tick, 0]
        for j in range(1, np_):
            total = total + sqp[tick, j]
        sqs[tick] = total
        sqz[tick, z] = total
        for j in range(1, nz):
            z_copy(tick, j).start()
        if tick == 0:
            @pl.when(c == 0)
            def _():
                for j in range(nz):
                    zo_copy(j).start()

    def scale_of(ref):
        total = ref[0]
        for j in range(1, nz):
            total = total + ref[j]
        sq = jnp.sum(jnp.sum(total, axis=1, keepdims=True), axis=0, keepdims=True)
        return 0.5 * jnp.sqrt(jnp.float32(3 * df * heads_all)) / jnp.sqrt(sq + 1e-06)

    def renorm(old, buf, scale, new, b):
        cols = slice(b * LANES, (b + 1) * LANES)
        for m in range(3):
            older = old[m, :, cols].astype(F32)
            moved = older + scale * gg[buf, b, m].astype(F32)
            was = jnp.sum(older * older, axis=0, keepdims=True)
            now = jnp.sum(moved * moved, axis=0, keepdims=True)
            factor = jnp.sqrt(was) / jnp.sqrt(now + 1e-06)
            new[m, :, cols] = (moved * factor).astype(BF16)

    def mix(tick, part, state, g):
        cols = slice(g * GROUP, (g + 1) * GROUP)
        q = qs[tick, part]
        p1 = jnp.dot(q, state[0, :, cols], preferred_element_type=F32)
        p3 = jnp.dot(q, state[1, :, cols], preferred_element_type=F32)
        pa[part, :, cols] = (p1 * sigmoid(p1) * p3).astype(BF16)

    tiles = tok // GROUP

    def mate_out(tick, i):
        at = pl.ds(i * GROUP, GROUP)
        return remote(os_.at[tick, at], out.at[tick, 0, core, at], os_s.at[tick, i], os_r.at[tick, i], mate)

    def apply_mate(tick, state):
        for i in range(tiles):
            at = slice(i * GROUP, (i + 1) * GROUP)
            o = lax.dot_general(pa[1, at], state[2], NT, preferred_element_type=F32)
            os_[tick, at, :] = o.astype(BF16)
            mate_out(tick, i).start()

    def apply_own(tick, state):
        o = lax.dot_general(pa[0], state[2], NT, preferred_element_type=F32)
        out[tick, 0, core] = o.astype(BF16)

    prepare(k0.at[0], v0.at[0], rate_columns(rt, 0, core), kt0, rv0, rvt0, tok)
    for g in range(ng):
        forward(k0.at[0], rv0, s0.at[0], tok, g)
        for m in order:
            part = grad(m, kt0, rvt0, tok, 2 * tok, g).astype(BF16).astype(F32)
            if m == order[0]:
                gx_copies[g].wait_recv()
            for b in blocks(g):
                gb[0, b, m] = (part[:, lanes(b)] + gxr[b, m].astype(F32)).astype(BF16)
        for b in blocks(g):
            rs_first(0, b)
        for b in blocks(g):
            rs_far(0, b)
    for cp in mate_copies:
        cp.start()
    loads[7].wait()
    loads[8].wait()
    prepare(k1.at[0], v1.at[0], rate_columns(rt, 1, core), kt1, rv1, rvt1, 0)
    for b in everyb:
        rs_second(0, b)
    for i in (0, 1, 2):
        mate_copies[i].wait_recv()
    prepare(k1.at[1], v1.at[1], rate_columns(rtp, 1, core), kt1, rv1, rvt1, tok)
    for b in everyb:
        rs_third(0, b)

    def hand_over(b):
        part = (b,) + chunk(0)
        return remote(gg.at[(0,) + part], gg.at[(1,) + part], ho_s.at[b], ho_r.at[b], twin)

    tile = jnp.zeros((8, 128), F32)
    for b in everyb:
        tile = tile + rs_last(0, b, 0)

        @pl.when(c == 0)
        def _():
            hand_over(b).start()

        ag_first(0, b)
    norm_first(0, tile)

    @pl.when(c == 0)
    def _():
        state_copies[order[2]].start()
        ag_second(0)

    @pl.when(c == 1)
    def _():
        for b in everyb:
            hand_over(b).wait_recv()
            ag_first(1, b)

    norm_second(0)

    @pl.when(c == 1)
    def _():
        ag_second(1)
        ag_third(1)
        for j in range(nz):
            zo_copy(j).wait_recv()
        for m in order:
            state_copies[m].wait_recv()

    @pl.when(c == 0)
    def _():
        fresh_load.wait()

    for g in range(ng):
        @pl.when(c == 1)
        def _():
            for b in blocks(g):
                ag_last(1, b)
            if g == 0:
                ag_second(0)
            scale = scale_of(sqo)
            for b in blocks(g):
                renorm(so, 1, scale, s2, b)

        forward(k1.at[0], rv1, s2, 0, g)
        forward(k1.at[1], rv1, s2, tok, g)
        for m in order:
            part = grad(m, kt1, rvt1, 0, 2 * tok, g).astype(BF16)
            for b in blocks(g):
                gb[1, b, m] = part[:, lanes(b)]
        for b in blocks(g):
            rs_first(1, b)
        for b in blocks(g):
            rs_far(1, b)
    for b in everyb:
        rs_second(1, b)
    ag_third(0)
    for b in everyb:
        rs_third(1, b)
    ag_fourth(0)
    tile = jnp.zeros((8, 128), F32)
    for b in everyb:
        tile = tile + rs_last(1, b, 2)
        ag_first(2, b)
    norm_first(1, tile)
    for j in range(1, nz):
        z_copy(0, j).wait_recv()
    loads[9].wait()
    mate_copies[3].wait_recv()
    scale = scale_of(sqz.at[0])
    for b in everyb:
        ag_last(0, b)
        renorm(s0.at[0], 0, scale, s1, b)
    for part in (0, 1):
        mix(0, part, s1, 0)
    ag_second(2)
    norm_second(1)
    for g in range(1, ng):
        for part in (0, 1):
            mix(0, part, s1, g)
    apply_mate(0, s1)
    ag_third(2)
    apply_own(0, s1)
    loads[10].wait()
    mate_copies[4].wait_recv()
    for j in range(1, nz):
        z_copy(1, j).wait_recv()
    scale = scale_of(sqz.at[1])
    for g in range(ng):
        for b in blocks(g):
            ag_last(2, b)
            renorm(s2, 2, scale, s3, b)
        for part in (1, 0):
            mix(1, part, s3, g)
    apply_mate(1, s3)
    apply_own(1, s3)

    for cp in gx_copies + mate_copies:
        cp.wait_send()
    for b in everyb:
        for tick in (0, 1):
            for hop in range(4):
                for d, s in sides:
                    rs_copy(tick, hop, d, s, b).wait_send()
        for buf in (0, 2):
            for hop in range(4):
                for d, s in sides:
                    ag_copy(buf, hop, d, s, b).wait_send()
    for tick in (0, 1):
        for j in range(1, np_):
            plane_copy(tick, j).wait_send()
        for j in range(1, nz):
            z_copy(tick, j).wait_send()

    @pl.when(c == 0)
    def _():
        for m in order:
            state_copies[m].wait_send()
        for b in everyb:
            hand_over(b).wait_send()
        for j in range(nz):
            zo_copy(j).wait_send()

    @pl.when(c == 1)
    def _():
        for b in everyb:
            for hop in range(4):
                for d, s in sides:
                    ag_copy(1, hop, d, s, b).wait_send()

    for tick in (0, 1):
        for i in range(tiles):
            mate_out(tick, i).wait()


def shards(mesh_shape, keys, values, queries, rates, state_in, fresh):
    nz, nh = mesh_shape["tok"] // 2, mesh_shape["head"]
    _, _, _, tok, dh = keys.shape
    df = state_in.shape[-1]
    heads_all = 2 * nh
    rows, nb = dh // nz, df // LANES
    cut = (nb, 3, dh, LANES)
    sizes = (nz, nh, tok, dh, df, heads_all)
    dma = pltpu.SemaphoreType.DMA

    def vm(*shape, dtype=BF16):
        return pltpu.VMEM(shape, dtype)

    both = 2 * tok
    state = (3, dh, df)
    scratch = [
        vm(2, tok, dh), vm(2, tok, dh), vm(2, tok, dh), vm(2, tok, dh), vm(2, 2, tok, dh), vm(2, tok, dh),
        vm(*rates.shape, dtype=F32), vm(*rates.shape, dtype=F32),
        vm(2, *state), vm(*state), vm(*state), vm(*state), vm(*state),
        vm(dh, both), vm(both, dh), vm(dh, both), vm(dh, both), vm(both, dh), vm(dh, both),
        vm(both, df), vm(both, df), vm(both, df), vm(2, tok, df),
        vm(*cut), vm(*cut), vm(2, *cut), vm(3, *cut),
        vm(2, 3, 2, nb, 3, rows, LANES), vm(2, 2, nb, 3, rows // 2, LANES), vm(2, 2, 2, nb, 3, rows, LANES),
        vm(2, 2 * nh, 8, 128, dtype=F32), vm(2, 8, 128, dtype=F32), vm(2, nz, 8, 128, dtype=F32), vm(nz, 8, 128, dtype=F32),
        dma((12,)), dma((5,)), dma((5,)), dma((3,)), dma((3,)),
        dma((2, 4, 2, nb)), dma((2, 4, 2, nb)), dma((3, 4, 2, nb)), dma((3, 4, 2, nb)),
        dma((nb,)), dma((nb,)), dma((3,)), dma((3,)),
        dma((2, 2 * nh)), dma((2, 2 * nh)), dma((2, nz)), dma((2, nz)), dma((nz,)), dma((nz,)),
        dma((2, tok // GROUP)), dma((2, tok // GROUP)),
    ]
    return pl.pallas_call(
        functools.partial(kernel, sizes),
        out_shape=pltpu.VMEM(queries.shape, BF16),
        in_specs=[pl.BlockSpec(memory_space=pltpu.HBM)] * 6,
        out_specs=pl.BlockSpec(memory_space=pltpu.VMEM),
        scratch_shapes=scratch,
        compiler_params=pltpu.CompilerParams(
            collective_id=0, has_side_effects=True, vmem_limit_bytes=40 * 1024 * 1024
        ),
        cost_estimate=pl.CostEstimate(flops=8_000_000_000, bytes_accessed=10_000_000, transcendentals=3_000_000),
    )(*(pltpu.with_memory_space_constraint(a, pltpu.HBM) for a in (keys, values, queries, rates, state_in, fresh)))


def solution(mesh):
    in_specs = (
        P(None, "ctx", "head", "tok", None),
        P(None, "ctx", "head", "tok", None),
        P(None, "ctx", "head", "tok", None),
        P(None, "ctx", "head", "tok"),
        P("ctx", "head", None, None, None),
        P("head", None, None, None),
    )
    return jax.shard_map(
        functools.partial(shards, dict(mesh.shape)),
        mesh=mesh,
        in_specs=in_specs,
        out_specs=P(None, "ctx", "head", "tok", None),
        check_vma=False,
    )
```

```python
import functools

import jax
import jax.numpy as jnp
from jax import lax
from jax.experimental import pallas as pl
from jax.experimental.pallas import tpu as pltpu
from jax.sharding import PartitionSpec as P

MESH = pl.DeviceIdType.MESH
F32, BF16 = jnp.float32, jnp.bfloat16
LANES, GROUP = 128, 256
NT = (((1,), (1,)), ((), ()))


def sigmoid(x):
    return 0.5 * jnp.tanh(0.5 * x) + 0.5


def kernel(
    sizes,
    keys, values, queries, rates, state_in, fresh,
    out,
    k0, v0, k1, v1, qs, os_, rt, rtp, s0, so, s1, s2, s3,
    kt0, rv0, rvt0, kt1, rv1, rvt1, act, d1, d3, pa,
    gx, gxr, gb, gg, rin, rhalf, rout,
    sqp, sqs, sqz, sqo,
    load_sem, xs, xr, gxs, gxrs, rs_s, rs_r, ag_s, ag_r, ho_s, ho_r, st_s, st_r,
    pp_s, pp_r, zz_s, zz_r, zo_s, zo_r, os_s, os_r,
):
    nz, nh, tok, dh, df, heads_all = sizes
    rows = dh // nz
    half = rows // 2
    nb, ng = df // LANES, df // GROUP
    per = nb // ng
    c, t, h = lax.axis_index("ctx"), lax.axis_index("tok"), lax.axis_index("head")
    z, core = t // 2, t % 2
    other = 1 - core
    np_ = 2 * nh
    me_p = h * 2 + core

    def zdev(step):
        return (c, lax.rem(z + step + nz, nz) * 2 + core, h)

    def pdev(j):
        p = lax.rem(me_p + j, np_)
        return (c, z * 2 + lax.rem(p, 2), p // 2)

    def odev(step):
        return (1 - c, lax.rem(z + step, nz) * 2 + core, h)

    mate = (c, z * 2 + other, h)
    twin = (1 - c, t, h)

    local = [
        (keys.at[0, 0, other], k0.at[1]),
        (state_in.at[0, other], s0.at[1]),
        (values.at[0, 0, other], v0.at[1]),
        (rates, rt),
        (keys.at[0, 0, core], k0.at[0]),
        (state_in.at[0, core], s0.at[0]),
        (values.at[0, 0, core], v0.at[0]),
        (keys.at[1, 0, core], k1.at[0]),
        (values.at[1, 0, core], v1.at[0]),
        (queries.at[0, 0, core], qs.at[0, 0]),
        (queries.at[1, 0, core], qs.at[1, 0]),
    ]
    loads = [pltpu.make_async_copy(a, b, load_sem.at[i]) for i, (a, b) in enumerate(local)]
    for i in (0, 1, 2, 3):
        loads[i].start()
    fresh_load = pltpu.make_async_copy(fresh.at[core], s2, load_sem.at[len(local)])

    barrier = pltpu.get_barrier_semaphore()
    for j in range(1, np_):
        pl.semaphore_signal(barrier, inc=1, device_id=pdev(j), device_id_type=MESH)
    for j in range(1, nz):
        pl.semaphore_signal(barrier, inc=1, device_id=zdev(j), device_id_type=MESH)
    for j in range(nz):
        pl.semaphore_signal(barrier, inc=1, device_id=odev(j), device_id_type=MESH)

    def remote(src, dst, ss, rs, dev):
        return pltpu.make_async_remote_copy(
            src_ref=src, dst_ref=dst, send_sem=ss, recv_sem=rs, device_id=dev, device_id_type=MESH
        )

    def rate_columns(ref, tick, head):
        row = jnp.where(head == 0, ref[tick, 0, 0:1, :], ref[tick, 0, 1:2, :])
        col = jnp.broadcast_to(row, (128, tok)).T
        return jnp.concatenate([col] * (dh // 128), axis=1)

    def prepare(k, v, col, kt, rv, rvt, lo):
        kt[:, lo:lo + tok] = k[...].T
        weighted = (v[...].astype(F32) * col).astype(BF16)
        rv[lo:lo + tok, :] = weighted
        rvt[:, lo:lo + tok] = weighted.T

    def forward(k, rv, state, lo, g):
        at, cols = slice(lo, lo + tok), slice(g * GROUP, (g + 1) * GROUP)
        kk = k[...]
        h1 = jnp.dot(kk, state[0, :, cols], preferred_element_type=F32)
        h3 = jnp.dot(kk, state[1, :, cols], preferred_element_type=F32)
        dact = jnp.dot(rv[at, :], state[2, :, cols], preferred_element_type=F32)
        sig = sigmoid(h1)
        hs = h1 * sig
        act[at, cols] = (hs * h3).astype(BF16)
        d3[at, cols] = (dact * hs).astype(BF16)
        d1[at, cols] = (dact * h3 * (sig + hs * (1.0 - sig))).astype(BF16)

    def grad(m, kt, rvt, lo, hi, g):
        left, right = ((kt, d1), (kt, d3), (rvt, act))[m]
        cols = slice(g * GROUP, (g + 1) * GROUP)
        return jnp.dot(left[:, lo:hi], right[lo:hi, cols], preferred_element_type=F32)

    def blocks(g):
        return range(g * per, (g + 1) * per)

    def lanes(b):
        return slice((b % per) * LANES, (b % per + 1) * LANES)

    order = (2, 0, 1)
    everyb = tuple(range(nb))

    for i in (4, 5, 6):
        loads[i].start()
    for i in (0, 1, 2, 3):
        loads[i].wait()
    prepare(k0.at[1], v0.at[1], rate_columns(rt, 0, other), kt0, rv0, rvt0, 0)
    for i in (7, 8, 9, 10):
        loads[i].start()

    @pl.when(c == 0)
    def _():
        fresh_load.start()

    for g in range(ng):
        forward(k0.at[1], rv0, s0.at[1], 0, g)
        for m in order:
            part = grad(m, kt0, rvt0, 0, tok, g).astype(BF16)
            for b in blocks(g):
                gx[b, m] = part[:, lanes(b)]

    pl.semaphore_wait(barrier, np_ - 1 + nz - 1 + nz)

    gx_copies = [
        remote(gx.at[pl.ds(g * per, per)], gxr.at[pl.ds(g * per, per)], gxs.at[g], gxrs.at[g], mate) for g in range(ng)
    ]
    for cp in gx_copies:
        cp.start()
    state_copies = {m: remote(s0.at[0, m], so.at[m], st_s.at[m], st_r.at[m], twin) for m in order}
    for i in (4, 5, 6):
        loads[i].wait()

    @pl.when(c == 0)
    def _():
        state_copies[order[0]].start()
        state_copies[order[1]].start()

    mate_copies = [
        remote(src, dst, xs.at[i], xr.at[i], mate)
        for i, (src, dst) in enumerate([
            (rates, rtp),
            (keys.at[1, 0, other], k1.at[1]),
            (values.at[1, 0, other], v1.at[1]),
            (queries.at[0, 0, other], qs.at[0, 1]),
            (queries.at[1, 0, other], qs.at[1, 1]),
        ])
    ]

    def chunk(owner_step, part=None):
        owner = lax.rem(z + owner_step + 2 * nz, nz)
        if part is None:
            return (slice(None), pl.ds(pl.multiple_of(owner * rows, rows), rows), slice(None))
        return (slice(None), pl.ds(pl.multiple_of(owner * rows + part * half, half), half), slice(None))

    sides = ((0, -1), (1, 1))

    def rs_copy(tick, hop, d, s, b):
        if hop == 0:
            src, dst, dev = gb.at[(tick, b) + chunk(3 * s)], rin.at[tick, 0, d, b], zdev(s)
        elif hop == 1:
            src, dst, dev = gb.at[(tick, b) + chunk(4, d)], rhalf.at[tick, d, b], zdev(3 * s)
        else:
            src, dst, dev = rout.at[tick, hop - 2, d, b], rin.at[tick, hop - 1, d, b], zdev(s)
        return remote(src, dst, rs_s.at[tick, hop, d, b], rs_r.at[tick, hop, d, b], dev)

    def rs_first(tick, b):
        for d, s in sides:
            rs_copy(tick, 0, d, s, b).start()

    def rs_far(tick, b):
        for d, s in sides:
            rs_copy(tick, 1, d, s, b).start()

    def rs_second(tick, b):
        for d, s in sides:
            rs_copy(tick, 0, d, s, b).wait_recv()
            own = gb[(tick, b) + chunk(2 * s)].astype(F32) + rin[tick, 0, d, b].astype(F32)
            rout[tick, 0, d, b] = own.astype(BF16)
            rs_copy(tick, 2, d, s, b).start()

    def rs_third(tick, b):
        for d, s in sides:
            rs_copy(tick, 2, d, s, b).wait_recv()
            rs_copy(tick, 1, d, s, b).wait_recv()
            own = gb[(tick, b) + chunk(s)].astype(F32) + rin[tick, 1, d, b].astype(F32)
            far = rhalf[tick, d, b].astype(F32)
            if d == 0:
                rout[tick, 1, d, b, :, 0:half, :] = (own[:, 0:half] + far).astype(BF16)
                rout[tick, 1, d, b, :, half:rows, :] = own[:, half:rows].astype(BF16)
            else:
                rout[tick, 1, d, b, :, 0:half, :] = own[:, 0:half].astype(BF16)
                rout[tick, 1, d, b, :, half:rows, :] = (own[:, half:rows] + far).astype(BF16)
            rs_copy(tick, 3, d, s, b).start()

    def rs_last(tick, b, buf):
        total = gb[(tick, b) + chunk(0)].astype(F32)
        for d, s in sides:
            rs_copy(tick, 3, d, s, b).wait_recv()
            total = total + rin[tick, 2, d, b].astype(F32)
        gg[(buf, b) + chunk(0)] = total.astype(BF16)
        square = total * total
        tile = jnp.zeros((8, 128), F32)
        for m in range(3):
            for i in range(0, rows, 8):
                tile = tile + square[m, i:i + 8]
        return tile

    def ag_copy(buf, hop, d, s, b):
        if hop == 0:
            part, dev = chunk(0), zdev(s)
        elif hop == 1:
            part, dev = chunk(-s), zdev(s)
        elif hop == 2:
            part, dev = chunk(-2 * s), zdev(s)
        elif buf == 0:
            part, dev = chunk(-3 * s, d), zdev(s)
        else:
            part, dev = chunk(-s, d), zdev(3 * s)
        part = (buf, b) + part
        return remote(gg.at[part], gg.at[part], ag_s.at[buf, hop, d, b], ag_r.at[buf, hop, d, b], dev)

    def ag_first(buf, b):
        for d, s in sides:
            ag_copy(buf, 0, d, s, b).start()

    def ag_second(buf):
        for g in range(ng):
            for b in blocks(g):
                for d, s in sides:
                    ag_copy(buf, 0, d, s, b).wait_recv()
                    ag_copy(buf, 1, d, s, b).start()
            if buf != 0:
                for b in blocks(g):
                    for d, s in sides:
                        ag_copy(buf, 3, d, s, b).start()

    def ag_third(buf):
        for b in everyb:
            for d, s in sides:
                ag_copy(buf, 1, d, s, b).wait_recv()
                ag_copy(buf, 2, d, s, b).start()

    def ag_fourth(buf):
        for b in everyb:
            for d, s in sides:
                ag_copy(buf, 2, d, s, b).wait_recv()
                ag_copy(buf, 3, d, s, b).start()

    def ag_last(buf, b):
        for d, s in sides:
            ag_copy(buf, 3, d, s, b).wait_recv()
            if buf != 0:
                ag_copy(buf, 2, d, s, b).wait_recv()

    def plane_copy(tick, j):
        return remote(sqp.at[tick, me_p], sqp.at[tick, me_p], pp_s.at[tick, j], pp_r.at[tick, j], pdev(j))

    def norm_first(tick, tile):
        sqp[tick, me_p] = tile
        for j in sorted(range(1, np_), key=lambda j: abs(j - nh)):
            plane_copy(tick, j).start()

    def z_copy(tick, j):
        return remote(sqs.at[tick], sqz.at[tick, z], zz_s.at[tick, j], zz_r.at[tick, j], zdev(j))

    def zo_copy(j):
        return remote(sqs.at[0], sqo.at[z], zo_s.at[j], zo_r.at[j], odev(j))

    def norm_second(tick):
        for j in range(1, np_):
            plane_copy(tick, j).wait_recv()
        total = sqp[tick, 0]
        for j in range(1, np_):
            total = total + sqp[tick, j]
        sqs[tick] = total
        sqz[tick, z] = total
        if tick == 0:
            @pl.when(c == 0)
            def _():
                for j in sorted(range(nz), key=lambda j: abs(j - nz // 2)):
                    zo_copy(j).start()
        for j in sorted(range(1, nz), key=lambda j: abs(j - nz // 2)):
            z_copy(tick, j).start()

    def scale_of(ref):
        total = ref[0]
        for j in range(1, nz):
            total = total + ref[j]
        sq = jnp.sum(jnp.sum(total, axis=1, keepdims=True), axis=0, keepdims=True)
        return 0.5 * jnp.sqrt(jnp.float32(3 * df * heads_all)) / jnp.sqrt(sq + 1e-06)

    def renorm(old, buf, scale, new, b):
        cols = slice(b * LANES, (b + 1) * LANES)
        for m in range(3):
            older = old[m, :, cols].astype(F32)
            moved = older + scale * gg[buf, b, m].astype(F32)
            was = jnp.sum(older * older, axis=0, keepdims=True)
            now = jnp.sum(moved * moved, axis=0, keepdims=True)
            factor = jnp.sqrt(was) / jnp.sqrt(now + 1e-06)
            new[m, :, cols] = (moved * factor).astype(BF16)

    def mix(tick, part, state, g):
        cols = slice(g * GROUP, (g + 1) * GROUP)
        q = qs[tick, part]
        p1 = jnp.dot(q, state[0, :, cols], preferred_element_type=F32)
        p3 = jnp.dot(q, state[1, :, cols], preferred_element_type=F32)
        pa[part, :, cols] = (p1 * sigmoid(p1) * p3).astype(BF16)

    tiles = tok // GROUP

    def mate_out(tick, i):
        at = pl.ds(i * GROUP, GROUP)
        return remote(os_.at[tick, at], out.at[tick, 0, core, at], os_s.at[tick, i], os_r.at[tick, i], mate)

    def apply_mate(tick, state):
        for i in range(tiles):
            at = slice(i * GROUP, (i + 1) * GROUP)
            o = lax.dot_general(pa[1, at], state[2], NT, preferred_element_type=F32)
            os_[tick, at, :] = o.astype(BF16)
            mate_out(tick, i).start()

    def apply_own(tick, state):
        o = lax.dot_general(pa[0], state[2], NT, preferred_element_type=F32)
        out[tick, 0, core] = o.astype(BF16)

    prepare(k0.at[0], v0.at[0], rate_columns(rt, 0, core), kt0, rv0, rvt0, tok)
    for g in range(ng):
        forward(k0.at[0], rv0, s0.at[0], tok, g)
        for m in order:
            part = grad(m, kt0, rvt0, tok, 2 * tok, g).astype(BF16).astype(F32)
            if m == order[0]:
                gx_copies[g].wait_recv()
            for b in blocks(g):
                gb[0, b, m] = (part[:, lanes(b)] + gxr[b, m].astype(F32)).astype(BF16)
        for b in blocks(g):
            rs_first(0, b)
        for b in blocks(g):
            rs_far(0, b)
    for cp in mate_copies:
        cp.start()
    loads[7].wait()
    loads[8].wait()
    prepare(k1.at[0], v1.at[0], rate_columns(rt, 1, core), kt1, rv1, rvt1, 0)
    for b in everyb:
        rs_second(0, b)
    for i in (0, 1, 2):
        mate_copies[i].wait_recv()
    prepare(k1.at[1], v1.at[1], rate_columns(rtp, 1, core), kt1, rv1, rvt1, tok)
    for b in everyb:
        rs_third(0, b)

    def hand_over(b):
        part = (b,) + chunk(0)
        return remote(gg.at[(0,) + part], gg.at[(1,) + part], ho_s.at[b], ho_r.at[b], twin)

    tile = jnp.zeros((8, 128), F32)
    for b in everyb:
        tile = tile + rs_last(0, b, 0)

        @pl.when(c == 0)
        def _():
            hand_over(b).start()

        ag_first(0, b)
    norm_first(0, tile)

    @pl.when(c == 0)
    def _():
        state_copies[order[2]].start()

    @pl.when(c == 1)
    def _():
        for b in everyb:
            hand_over(b).wait_recv()
            ag_first(1, b)

    norm_second(0)

    @pl.when(c == 0)
    def _():
        ag_second(0)

    @pl.when(c == 1)
    def _():
        ag_second(1)
        ag_third(1)
        for j in range(nz):
            zo_copy(j).wait_recv()
        for m in order:
            state_copies[m].wait_recv()

    @pl.when(c == 0)
    def _():
        fresh_load.wait()

    for g in range(ng):
        @pl.when(c == 1)
        def _():
            for b in blocks(g):
                ag_last(1, b)
            if g == 0:
                ag_second(0)
            scale = scale_of(sqo)
            for b in blocks(g):
                renorm(so, 1, scale, s2, b)

        forward(k1.at[0], rv1, s2, 0, g)
        forward(k1.at[1], rv1, s2, tok, g)
        for m in order:
            part = grad(m, kt1, rvt1, 0, 2 * tok, g).astype(BF16)
            for b in blocks(g):
                gb[1, b, m] = part[:, lanes(b)]
        for b in blocks(g):
            rs_first(1, b)
        for b in blocks(g):
            rs_far(1, b)
    for b in everyb:
        rs_second(1, b)
    ag_third(0)
    for b in everyb:
        rs_third(1, b)
    ag_fourth(0)
    tile = jnp.zeros((8, 128), F32)
    for b in everyb:
        tile = tile + rs_last(1, b, 2)
        ag_first(2, b)
    norm_first(1, tile)
    for j in range(1, nz):
        z_copy(0, j).wait_recv()
    loads[9].wait()
    mate_copies[3].wait_recv()
    scale = scale_of(sqz.at[0])
    for b in everyb:
        ag_last(0, b)
        renorm(s0.at[0], 0, scale, s1, b)
    for part in (0, 1):
        mix(0, part, s1, 0)
    ag_second(2)
    norm_second(1)
    for g in range(1, ng):
        for part in (0, 1):
            mix(0, part, s1, g)
    apply_mate(0, s1)
    ag_third(2)
    apply_own(0, s1)
    loads[10].wait()
    mate_copies[4].wait_recv()
    for j in range(1, nz):
        z_copy(1, j).wait_recv()
    scale = scale_of(sqz.at[1])
    for g in range(ng):
        for b in blocks(g):
            ag_last(2, b)
            renorm(s2, 2, scale, s3, b)
        for part in (1, 0):
            mix(1, part, s3, g)
    apply_mate(1, s3)
    apply_own(1, s3)

    for cp in gx_copies + mate_copies:
        cp.wait_send()
    for b in everyb:
        for tick in (0, 1):
            for hop in range(4):
                for d, s in sides:
                    rs_copy(tick, hop, d, s, b).wait_send()
        for buf in (0, 2):
            for hop in range(4):
                for d, s in sides:
                    ag_copy(buf, hop, d, s, b).wait_send()
    for tick in (0, 1):
        for j in range(1, np_):
            plane_copy(tick, j).wait_send()
        for j in range(1, nz):
            z_copy(tick, j).wait_send()

    @pl.when(c == 0)
    def _():
        for m in order:
            state_copies[m].wait_send()
        for b in everyb:
            hand_over(b).wait_send()
        for j in range(nz):
            zo_copy(j).wait_send()

    @pl.when(c == 1)
    def _():
        for b in everyb:
            for hop in range(4):
                for d, s in sides:
                    ag_copy(1, hop, d, s, b).wait_send()

    for tick in (0, 1):
        for i in range(tiles):
            mate_out(tick, i).wait()


def shards(mesh_shape, keys, values, queries, rates, state_in, fresh):
    nz, nh = mesh_shape["tok"] // 2, mesh_shape["head"]
    _, _, _, tok, dh = keys.shape
    df = state_in.shape[-1]
    heads_all = 2 * nh
    rows, nb = dh // nz, df // LANES
    cut = (nb, 3, dh, LANES)
    sizes = (nz, nh, tok, dh, df, heads_all)
    dma = pltpu.SemaphoreType.DMA

    def vm(*shape, dtype=BF16):
        return pltpu.VMEM(shape, dtype)

    both = 2 * tok
    state = (3, dh, df)
    scratch = [
        vm(2, tok, dh), vm(2, tok, dh), vm(2, tok, dh), vm(2, tok, dh), vm(2, 2, tok, dh), vm(2, tok, dh),
        vm(*rates.shape, dtype=F32), vm(*rates.shape, dtype=F32),
        vm(2, *state), vm(*state), vm(*state), vm(*state), vm(*state),
        vm(dh, both), vm(both, dh), vm(dh, both), vm(dh, both), vm(both, dh), vm(dh, both),
        vm(both, df), vm(both, df), vm(both, df), vm(2, tok, df),
        vm(*cut), vm(*cut), vm(2, *cut), vm(3, *cut),
        vm(2, 3, 2, nb, 3, rows, LANES), vm(2, 2, nb, 3, rows // 2, LANES), vm(2, 2, 2, nb, 3, rows, LANES),
        vm(2, 2 * nh, 8, 128, dtype=F32), vm(2, 8, 128, dtype=F32), vm(2, nz, 8, 128, dtype=F32), vm(nz, 8, 128, dtype=F32),
        dma((12,)), dma((5,)), dma((5,)), dma((3,)), dma((3,)),
        dma((2, 4, 2, nb)), dma((2, 4, 2, nb)), dma((3, 4, 2, nb)), dma((3, 4, 2, nb)),
        dma((nb,)), dma((nb,)), dma((3,)), dma((3,)),
        dma((2, 2 * nh)), dma((2, 2 * nh)), dma((2, nz)), dma((2, nz)), dma((nz,)), dma((nz,)),
        dma((2, tok // GROUP)), dma((2, tok // GROUP)),
    ]
    return pl.pallas_call(
        functools.partial(kernel, sizes),
        out_shape=pltpu.VMEM(queries.shape, BF16),
        in_specs=[pl.BlockSpec(memory_space=pltpu.HBM)] * 6,
        out_specs=pl.BlockSpec(memory_space=pltpu.VMEM),
        scratch_shapes=scratch,
        compiler_params=pltpu.CompilerParams(
            collective_id=0, has_side_effects=True, vmem_limit_bytes=40 * 1024 * 1024
        ),
        cost_estimate=pl.CostEstimate(flops=8_000_000_000, bytes_accessed=10_000_000, transcendentals=3_000_000),
    )(*(pltpu.with_memory_space_constraint(a, pltpu.HBM) for a in (keys, values, queries, rates, state_in, fresh)))


def solution(mesh):
    in_specs = (
        P(None, "ctx", "head", "tok", None),
        P(None, "ctx", "head", "tok", None),
        P(None, "ctx", "head", "tok", None),
        P(None, "ctx", "head", "tok"),
        P("ctx", "head", None, None, None),
        P("head", None, None, None),
    )
    return jax.shard_map(
        functools.partial(shards, dict(mesh.shape)),
        mesh=mesh,
        in_specs=in_specs,
        out_specs=P(None, "ctx", "head", "tok", None),
        check_vma=False,
    )
```
